1024 devices in a mesh: gx: 16 (over y, core), gy: 4 (over z_lo), mz: 16 (over z_hi, x).
Axes of the slice: x: 4, y: 8, z: 16 (z_hi: 4, z_lo: 4; z = z_hi * 4 + z_lo), core: 2. Of those that a mesh axis runs over, the one named last changes fastest.
Arguments:
- spectra: bfloat16 [128, 32, 832, 128], P('gx', 'gy', 'mz'), may hold values from 1 to 100
- block_ids: int32 [16, 4, 832], P('gx', 'gy', 'mz'), may hold values from 0 to 97, as said below
- counts: int32 [16, 4, 16], P('gx', 'gy', 'mz'), may hold values from 6 to 52, as said below
- loadings: float32 [128, 32, 64], P('gx', 'gy'), may hold values from 0.15 to 1.5
- components: float32 [64, 200704], P(None, 'mz'), may hold values from 0.15 to 1.5
Outputs:
- w_next: float32 [128, 32, 64], P('gx', 'gy')
- h_next: float32 [64, 200704], P(('gx', 'gy'), 'mz')
The draws below stay inside these ranges and needn't reach their ends.
Inputs may be any that keep to these rules, and one draw needn't show every extreme that they name: `block_ids`: the 52 numbers of one tile and slab are distinct; the first counts of them are the occupied blocks, the others are unused. `counts`: some tile and slab has exactly 52 occupied slots.
All inputs are finite; a program needn't handle non-finite values.
Results may differ from the reference program's by a relative error of at most 0.0003.
Values may be sent and summed in bfloat16 or wider, within the bound.
No kernel may reach another device: no remote copies, remote signals or barrier semaphores. Data moves between devices by JAX's collectives and lax.ppermute only.
A program may use at most 32 MiB of HBM per device.

```python
import math
import jax
import jax.numpy as jnp
from jax import lax

K = 64
NB = 98
TX = 8
TY = 8
CAP = 52
IX = 128
IY = 32
BINS = 200704
N_GX = 16
N_GY = 4
N_MZ = 16


def draw_block_ids(key, part):
    key = jax.random.fold_in(key, 5)
    owners = N_GX * N_GY * N_MZ
    subkeys = jax.random.split(key, owners)
    chosen = jax.vmap(lambda subkey: jax.random.permutation(subkey, NB)[:CAP])(subkeys)
    return chosen.reshape(N_GX, N_GY, N_MZ * CAP).astype(jnp.int32)


def draw_counts(key, part):
    key = jax.random.fold_in(key, 9)
    first_key, second_key = jax.random.split(key)
    owners = N_GX * N_GY * N_MZ
    shifts = jax.random.randint(first_key, (owners,), 0, 4)
    filled = jnp.maximum(jnp.right_shift(jnp.full((owners,), CAP, jnp.int32), shifts), 1)
    fullest = jax.random.randint(second_key, (), 0, owners)
    filled = jnp.where(jnp.arange(owners) == fullest, CAP, filled)
    return filled.reshape(N_GX, N_GY, N_MZ).astype(jnp.int32)


def steps_of(rng, dims, shards, smallest, largest):
    def one(position, blocks):
        draws = jax.random.uniform(jax.random.fold_in(jax.random.fold_in(rng, 6), position), (blocks,), jnp.float32, smallest / len(shards), largest / len(shards))
        return jnp.repeat(jnp.exp(draws), dims[position] // blocks).reshape((-1,) + (1,) * (len(dims) - position - 1))

    gain = one(*shards[0])
    for cut in shards[1:]:
        gain = gain * one(*cut)
    return gain


def setup_inputs(seed: int = 0) -> dict:
    splits = jax.random.split(jax.random.key(seed), 6)
    spectra = jnp.clip(jnp.exp(math.log(100.0) - 4.6051702 * jax.random.uniform(splits[0], (IX, IY, N_MZ * CAP, 128), jnp.float32) ** steps_of(splits[0], (IX, IY, N_MZ * CAP, 128), ((0, 16), (1, 4), (2, 16)), -0.2, 0.2)), 1.0, 100.0).astype(jnp.bfloat16)
    block_ids = draw_block_ids(jax.random.fold_in(splits[5], 71), 0)
    counts = draw_counts(jax.random.fold_in(splits[5], 71), 0)
    loadings = jnp.clip(jnp.exp(math.log(1.5) - 2.3025851 * jax.random.uniform(splits[3], (IX, IY, K), jnp.float32) ** steps_of(splits[3], (IX, IY, K), ((0, 16), (1, 4)), -0.2, 0.2)), 0.15, 1.5)
    components = jnp.clip(jnp.exp(math.log(1.5) - 2.3025851 * jax.random.uniform(splits[4], (K, BINS), jnp.float32) ** steps_of(splits[4], (K, BINS), ((1, 16),), -0.2, 0.2)), 0.15, 1.5)
    return dict(spectra=spectra, block_ids=block_ids, counts=counts, loadings=loadings, components=components)


tv_edge = 0.1
tv_share = 0.1


def smoothing(padded):
    centre = padded[1:-1, 1:-1]
    smooth_num = jnp.zeros_like(centre)
    smooth_den = jnp.zeros_like(centre)
    for beside in (padded[2:, 1:-1], padded[:-2, 1:-1], padded[1:-1, 2:], padded[1:-1, :-2]):
        edge_weight = 1.0 / (jnp.abs(centre - beside) + tv_edge)
        smooth_num = smooth_num + edge_weight * beside
        smooth_den = smooth_den + edge_weight * centre
    return smooth_num, smooth_den


def tile_pieces(spectra, block_ids, counts, loadings, tile_index):
    row_tile = (tile_index // N_GY).astype(jnp.int32)
    col_tile = (tile_index % N_GY).astype(jnp.int32)
    anchor = jnp.zeros((), jnp.int32)
    tile_data = lax.dynamic_slice(spectra, (row_tile * TX, col_tile * TY, anchor, anchor), (TX, TY, N_MZ * CAP, 128))
    tile_data = tile_data.reshape(TX * TY, N_MZ, CAP * 128).astype(jnp.float32)
    tile_w = lax.dynamic_slice(loadings, (row_tile * TX, col_tile * TY, anchor), (TX, TY, K)).reshape(TX * TY, K)
    slot_ids = lax.dynamic_slice(block_ids, (row_tile, col_tile, anchor), (1, 1, N_MZ * CAP)).reshape(N_MZ, CAP)
    slot_live = lax.dynamic_slice(counts, (row_tile, col_tile, anchor), (1, 1, N_MZ)).reshape(N_MZ)
    is_live = jnp.arange(CAP, dtype=jnp.int32)[None, :] < slot_live[:, None]
    placing = jnp.logical_and(slot_ids[:, :, None] == jnp.arange(NB, dtype=jnp.int32)[None, None, :], is_live[:, :, None])
    return tile_data, tile_w, placing.astype(jnp.float32)


def reference(spectra, block_ids, counts, loadings, components):
    tiles = N_GX * N_GY
    tile_list = jnp.arange(tiles, dtype=jnp.int32)

    def accumulate(total, tile_index):
        tile_data, tile_w, placing = tile_pieces(spectra, block_ids, counts, loadings, tile_index)
        w_low = tile_w.astype(jnp.bfloat16).astype(jnp.float32)
        partial_value = jnp.einsum("pk,pmc->mkc", w_low, tile_data).reshape(N_MZ, K, CAP, 128)
        placed = jnp.einsum("mkcb,mcn->mknb", partial_value, placing, precision=lax.Precision.HIGHEST)
        return total + placed.reshape(N_MZ, K, NB * 128), None

    start_total = jnp.zeros((N_MZ, K, NB * 128), jnp.float32)
    total, unused = lax.scan(accumulate, start_total, tile_list)
    numer = total.transpose(1, 0, 2).reshape(K, BINS)
    loadings_low = loadings.reshape(IX * IY, K).astype(jnp.bfloat16)
    gram = jnp.dot(loadings_low.T, loadings_low, preferred_element_type=jnp.float32)
    h_next = components * numer / jnp.dot(gram, components, precision=lax.Precision.HIGHEST)
    h_low = h_next.astype(jnp.bfloat16)
    spec_gram = jnp.dot(h_low, h_low.T, preferred_element_type=jnp.float32)
    h_slabs = h_low.astype(jnp.float32).reshape(K, N_MZ, NB, 128)

    def project(tile_index):
        tile_data, tile_w, placing = tile_pieces(spectra, block_ids, counts, loadings, tile_index)
        picked = jnp.einsum("mcn,kmnb->mkcb", placing, h_slabs).reshape(N_MZ, K, CAP * 128)
        return jnp.einsum("pmc,mkc->pk", tile_data, picked)

    per_tile = lax.map(project, tile_list)
    cross = per_tile.reshape(N_GX, N_GY, TX, TY, K).transpose(0, 2, 1, 3, 4).reshape(IX, IY, K)
    padded = jnp.pad(loadings, ((1, 1), (1, 1), (0, 0)))
    smooth_num, smooth_den = smoothing(padded)
    tv_strength = tv_share * BINS
    fitted = jnp.dot(loadings.reshape(IX * IY, K), spec_gram, precision=lax.Precision.HIGHEST).reshape(IX, IY, K)
    w_next = loadings * (cross + tv_strength * smooth_num) / (fitted + tv_strength * smooth_den)
    return w_next, h_next
```

```python
import functools
import jax
import jax.numpy as jnp
from jax import lax
from jax.experimental import pallas as pl
from jax.experimental.pallas import tpu as pltpu
from jax.sharding import Mesh, PartitionSpec as P

tv_edge = 0.1
tv_share = 0.1
LANE = 128
VMEM_LIMIT = 48 * 1024 * 1024
F32 = jnp.float32
BF16 = jnp.bfloat16


def params():
    return pltpu.CompilerParams(vmem_limit_bytes=VMEM_LIMIT)


def vmem():
    return pl.BlockSpec(memory_space=pltpu.VMEM)


def smem():
    return pl.BlockSpec(memory_space=pltpu.SMEM)


def iota(shape, dim):
    return lax.broadcasted_iota(jnp.int32, shape, dim)


def nt(a, b):
    return lax.dot_general(a, b, (((1,), (1,)), ((), ())), preferred_element_type=F32)


def numer_kernel(where_ref, ids_ref, count_ref, x_ref, w_ref, out_ref, dense_ref, wide_ref):
    tile, slots, lane = x_ref.shape
    pitch = wide_ref.shape[0] // tile
    half_blocks = dense_ref.shape[0]
    comps = w_ref.shape[1]
    rows = out_ref.shape[0]
    me = where_ref[0]
    last = rows // 8 - 1

    w = w_ref[...]
    w_low = w.astype(BF16)
    w_two = jnp.concatenate([w_low, w_low], axis=0)
    row = iota((rows, comps), 0)
    pick = jnp.where(iota((rows, comps), 1) == 4 * (row // 8) + row % 4, 1.0, 0.0).astype(BF16)
    spread = nt(pick, w_two)
    row = iota((rows, 2 * tile), 0)
    same_half = (row // 4) % 2 == iota((rows, 2 * tile), 1) // tile
    left = jnp.where(same_half, spread, 0.0).astype(BF16)

    dense_ref[...] = jnp.zeros_like(dense_ref)
    for p in range(tile):
        wide_ref[p * pitch : p * pitch + slots, :] = x_ref[p].astype(F32)

    def place(s, carry):
        block = ids_ref[s]
        high = block // half_blocks
        rows_of_slot = wide_ref[pl.ds(s, tile, stride=pitch), :].astype(BF16)
        dense_ref[block - high * half_blocks, pl.ds(pl.multiple_of(high * tile, tile), tile), :] = rows_of_slot
        return carry

    lax.fori_loop(0, count_ref[0], place, 0)

    for j in range(half_blocks):
        out_ref[:, j * lane : (j + 1) * lane] = jnp.dot(left, dense_ref[j], preferred_element_type=F32)

    base = half_blocks * lane
    out_ref[:, base : base + 3 * lane] = jnp.zeros((rows, 3 * lane), F32)
    out_ref[:, base : base + comps] = jnp.dot(left, w_two, preferred_element_type=F32)

    pair = jnp.concatenate([w, w], axis=1)
    first = iota((8, lane), 1) < comps

    @pl.when(me < last)
    def _():
        at = pl.ds(pl.multiple_of(8 * (me + 1), 8), 8)
        out_ref[at, base + lane : base + 2 * lane] += jnp.where(first, pair[tile - 8 :], 0.0)

    @pl.when(me > 0)
    def _():
        at = pl.ds(pl.multiple_of(8 * (me - 1), 8), 8)
        out_ref[at, base + lane : base + 2 * lane] += jnp.where(first, 0.0, pair[:8])

    heads = jnp.concatenate([pair[8 * i : 8 * i + 1] for i in range(8)], axis=0)
    tails = jnp.concatenate([pair[8 * i + 7 : 8 * i + 8] for i in range(8)], axis=0)
    out_ref[pl.ds(pl.multiple_of(8 * me, 8), 8), base + 2 * lane :] = jnp.where(first, heads, tails)


def spectra_kernel(tv_strength, where_ref, parts_ref, comps_ref, w_ref, h_low_ref, h_ref, tv_num_ref, tv_den_ref):
    lane = LANE
    half_blocks = h_low_ref.shape[1] // lane
    base = half_blocks * lane
    comps = comps_ref.shape[0]
    me, side = where_ref[0], where_ref[1]
    sides = parts_ref.shape[0]

    def total(start):
        block = parts_ref[0, :, pl.ds(start, lane)]
        for i in range(1, sides):
            block = block + parts_ref[i, :, pl.ds(start, lane)]
        return block

    gram = jnp.transpose(total(base))[:comps, :]
    weights = [jnp.broadcast_to(gram[:, i : i + 1], (comps, lane)) for i in range(4)]
    odd = me % 2
    own_at = pl.ds(pl.multiple_of(8 * (me // 2), 8), 8)
    top = iota((8, lane), 0) < 4

    def block_step(j, carry):
        numer = total(pl.multiple_of(j * lane, lane))
        denominators = []
        own = []
        for half in range(2):
            at = pl.ds(pl.multiple_of((half * half_blocks + j) * lane, lane), lane)
            block = comps_ref[:, at]
            for i in range(4):
                denominators.append(jnp.sum(block * weights[i], axis=0, keepdims=True))
            own.append(comps_ref[own_at, at])
        denominator = jnp.concatenate(denominators, axis=0)
        own_rows = jnp.where(top, pltpu.roll(own[0], 4 * odd, 0), pltpu.roll(own[1], 4 * (1 - odd), 0))
        h = own_rows * numer / denominator
        h_low_ref[:, pl.ds(pl.multiple_of(j * lane, lane), lane)] = h.astype(BF16)
        turned = pltpu.roll(h, lax.rem(8 - side, 8), 0)
        h_ref[:, pl.ds(pl.multiple_of(j * lane, lane), lane)] = turned[0:1]
        h_ref[:, pl.ds(pl.multiple_of((half_blocks + j) * lane, lane), lane)] = turned[4:5]
        return carry

    lax.fori_loop(0, half_blocks, block_step, 0)

    rim = parts_ref[side, :, base + lane : base + 2 * lane]
    above, below = rim[:, :comps], rim[:, comps:]
    before = parts_ref[jnp.maximum(side - 1, 0), :, base + 2 * lane :][:, comps:]
    before = jnp.where(side > 0, before, 0.0)
    after = parts_ref[jnp.minimum(side + 1, sides - 1), :, base + 2 * lane :][:, :comps]
    after = jnp.where(side < sides - 1, after, 0.0)
    spot = iota((8, comps), 0)
    rows = [w_ref[8 * i : 8 * i + 8, :] for i in range(8)]
    for i in range(8):
        centre = rows[i]
        beside = (
            rows[i + 1] if i < 7 else below,
            rows[i - 1] if i > 0 else above,
            jnp.where(spot == 7, after[i : i + 1], pltpu.roll(centre, 7, 0)),
            jnp.where(spot == 0, before[i : i + 1], pltpu.roll(centre, 1, 0)),
        )
        num = jnp.zeros_like(centre)
        den = jnp.zeros_like(centre)
        for q in beside:
            edge_weight = 1.0 / (jnp.abs(centre - q) + tv_edge)
            num = num + edge_weight * q
            den = den + edge_weight * centre
        tv_num_ref[8 * i : 8 * i + 8, :] = tv_strength * num
        tv_den_ref[8 * i : 8 * i + 8, :] = tv_strength * den


def project_kernel(h_ref, dense_ref, out_ref):
    half_blocks, two_tiles, lane = dense_ref.shape
    rows = h_ref.shape[0]
    copies, tile, _ = out_ref.shape
    comps = rows // 2
    cross = jnp.zeros((two_tiles, rows), F32)
    spec = jnp.zeros((rows, rows), F32)
    for j in range(half_blocks):
        block = h_ref[:, j * lane : (j + 1) * lane]
        cross = cross + nt(dense_ref[j], block)
        spec = spec + nt(block, block)
    row, col = iota((two_tiles, rows), 0), iota((two_tiles, rows), 1)
    cross = jnp.where(row // tile == (col // 4) % 2, cross, 0.0)
    cross = cross[:tile] + cross[tile:]
    row, col = iota((rows, rows), 0), iota((rows, rows), 1)
    spec = jnp.where((row // 4) % 2 == (col // 4) % 2, spec, 0.0)
    name = 4 * (row // 8) + row % 4
    to_low = jnp.where(col == name, 1.0, 0.0)
    to_high = jnp.where(col == name + comps, 1.0, 0.0)
    spec = lax.dot_general(
        to_low, spec, (((0,), (0,)), ((), ())), preferred_element_type=F32, precision=lax.Precision.HIGHEST
    )[:comps]
    both = jnp.dot(cross, to_low, preferred_element_type=F32, precision=lax.Precision.HIGHEST) + jnp.dot(
        spec, to_high, preferred_element_type=F32, precision=lax.Precision.HIGHEST
    )
    for i in range(copies):
        out_ref[i] = both


def sum_kernel(parts_ref, out_ref):
    block = parts_ref[0]
    for i in range(1, parts_ref.shape[0]):
        block = block + parts_ref[i]
    out_ref[...] = block


def loadings_kernel(parts_ref, w_ref, tv_num_ref, tv_den_ref, out_ref):
    comps = w_ref.shape[1]
    block = parts_ref[0]
    for i in range(1, parts_ref.shape[0]):
        block = block + parts_ref[i]
    w = w_ref[...]
    fitted = jnp.dot(w, block, preferred_element_type=F32, precision=lax.Precision.HIGHEST)
    fitted = pltpu.roll(fitted, comps, 1)[:, :comps]
    out_ref[...] = w * (block[:, :comps] + tv_num_ref[...]) / (fitted + tv_den_ref[...])


def local(spectra, block_ids, counts, loadings, components):
    tile_x, tile_y, slot_count, lane = spectra.shape
    tile = tile_x * tile_y
    comps = loadings.shape[2]
    slab_bins = components.shape[1]
    half_blocks = slab_bins // lane // 2
    half_bins = half_blocks * lane
    rows = 2 * comps
    width = half_bins + 3 * lane
    here = jnp.stack([lax.axis_index("gx"), lax.axis_index("gy")]).astype(jnp.int32)
    pixels = spectra.reshape(tile, slot_count, lane)
    w = loadings.reshape(tile, comps)
    pitch = -(-slot_count // 8) * 8

    num_term, dense = pl.pallas_call(
        numer_kernel,
        out_shape=(
            jax.ShapeDtypeStruct((rows, width), F32),
            jax.ShapeDtypeStruct((half_blocks, 2 * tile, lane), BF16),
        ),
        in_specs=[smem(), smem(), smem(), vmem(), vmem()],
        out_specs=(vmem(), vmem()),
        scratch_shapes=[pltpu.VMEM((tile * pitch, lane), F32)],
        compiler_params=params(),
        name="numer",
    )(here, block_ids.reshape(slot_count), counts.reshape(1), pixels, w)

    reduced = lax.psum_scatter(num_term, "gx", scatter_dimension=0, tiled=True)
    parts = lax.all_gather(reduced, "gy", axis=0)

    tv_strength = tv_share * slab_bins * lax.axis_size(("w", "x"))
    h_low, h_next, tv_num, tv_den = pl.pallas_call(
        functools.partial(spectra_kernel, tv_strength),
        out_shape=(
            jax.ShapeDtypeStruct((8, half_bins), BF16),
            jax.ShapeDtypeStruct((1, slab_bins), F32),
            jax.ShapeDtypeStruct((tile, comps), F32),
            jax.ShapeDtypeStruct((tile, comps), F32),
        ),
        in_specs=[smem(), vmem(), vmem(), vmem()],
        out_specs=(vmem(),) * 4,
        compiler_params=params(),
        name="spectra",
    )(here, parts, components, w)

    h_whole = lax.all_gather(h_low, "gx", axis=0, tiled=True)

    copies = lax.axis_size("x")
    both = pl.pallas_call(
        project_kernel,
        out_shape=jax.ShapeDtypeStruct((copies, tile, 2 * comps), F32),
        in_specs=[vmem(), vmem()],
        out_specs=vmem(),
        compiler_params=params(),
        name="project",
    )(h_whole, dense)

    both = lax.all_to_all(both, "x", 0, 0, tiled=True)
    both = pl.pallas_call(
        sum_kernel,
        out_shape=jax.ShapeDtypeStruct((tile, 2 * comps), F32),
        in_specs=[vmem()],
        out_specs=vmem(),
        compiler_params=params(),
        name="sum",
    )(both)
    both = lax.all_gather(both, "w", axis=0)
    w_next = pl.pallas_call(
        loadings_kernel,
        out_shape=jax.ShapeDtypeStruct((tile, comps), F32),
        in_specs=[vmem()] * 4,
        out_specs=vmem(),
        compiler_params=params(),
        name="loadings",
    )(both, w, tv_num, tv_den)
    return (w_next.reshape(tile_x, tile_y, comps), h_next)


def solution(mesh):
    gx, gy, mz = mesh.devices.shape
    fine = Mesh(mesh.devices.reshape(gx, gy, 4, mz // 4), ("gx", "gy", "w", "x"))
    slabs = ("w", "x")
    in_specs = (
        P("gx", "gy", slabs, None),
        P("gx", "gy", slabs),
        P("gx", "gy", slabs),
        P("gx", "gy", None),
        P(None, slabs),
    )
    out_specs = (P("gx", "gy", None), P(("gx", "gy"), slabs))
    return jax.shard_map(local, mesh=fine, in_specs=in_specs, out_specs=out_specs, check_vma=False)
```

```python
import functools
import jax
import jax.numpy as jnp
from jax import lax
from jax.experimental import pallas as pl
from jax.experimental.pallas import tpu as pltpu
from jax.sharding import Mesh, PartitionSpec as P

tv_edge = 0.1
tv_share = 0.1
LANE = 128
VMEM_LIMIT = 48 * 1024 * 1024
F32 = jnp.float32
BF16 = jnp.bfloat16


def params():
    return pltpu.CompilerParams(vmem_limit_bytes=VMEM_LIMIT)


def vmem():
    return pl.BlockSpec(memory_space=pltpu.VMEM)


def smem():
    return pl.BlockSpec(memory_space=pltpu.SMEM)


def iota(shape, dim):
    return lax.broadcasted_iota(jnp.int32, shape, dim)


def nt(a, b):
    return lax.dot_general(a, b, (((1,), (1,)), ((), ())), preferred_element_type=F32)


LOG_LOW = 3.25
LOG_STEPS = 5950.0
GRAM_SCALE = 64.0
OFFSET = 32768


def encode(value):
    steps = (jnp.log2(jnp.maximum(value, 1.0)) - LOG_LOW) * LOG_STEPS
    code = jnp.where(value > 0.0, jnp.maximum(steps, 0.0) + 1.5, 0.0).astype(jnp.int32)
    return (jnp.minimum(code, 65535) - OFFSET).astype(jnp.int16)


def decode(code):
    steps = code.astype(jnp.int32).astype(F32) + float(OFFSET)
    return jnp.where(steps > 0.0, jnp.exp2((steps - 1.0) * (1.0 / LOG_STEPS) + LOG_LOW), 0.0)


def numer_kernel(where_ref, ids_ref, count_ref, x_ref, w_ref, send_ref, keep_ref, dense_ref):
    tile_x, slots, tile_y, lane = x_ref.shape
    tile = tile_x * tile_y
    half_blocks = dense_ref.shape[0]
    comps = w_ref.shape[1]
    rows = send_ref.shape[0]
    core = where_ref[2]

    w = w_ref[...]
    w_low = w.astype(BF16)
    w_two = jnp.concatenate([w_low, w_low], axis=0)
    row = iota((2 * rows, comps), 0)
    row_core = jnp.where(row < rows, 1 - core, core)
    row = row % rows
    name = 8 * (row // 8) + 4 * row_core + row % 4
    pick = jnp.where(iota((2 * rows, comps), 1) == name, 1.0, 0.0).astype(BF16)
    spread = nt(pick, w_two)
    row = iota((2 * rows, 2 * tile), 0)
    same_half = (row // 4) % 2 == iota((2 * rows, 2 * tile), 1) // tile
    left = jnp.where(same_half, spread, 0.0).astype(BF16)

    dense_ref[...] = jnp.zeros_like(dense_ref)

    def place(s, carry):
        block = ids_ref[s]
        high = block // half_blocks
        rows_of_slot = x_ref[:, s].astype(F32).reshape(tile, lane).astype(BF16)
        dense_ref[block - high * half_blocks, pl.ds(pl.multiple_of(high * tile, tile), tile), :] = rows_of_slot
        return carry

    lax.fori_loop(0, count_ref[0], place, 0)

    for j in range(half_blocks):
        product = jnp.dot(left, dense_ref[j], preferred_element_type=F32)
        send_ref[:, j * lane : (j + 1) * lane] = product[:rows]
        keep_ref[:, j * lane : (j + 1) * lane] = product[rows:]

    base = half_blocks * lane
    product = jnp.dot(left, w_two, preferred_element_type=F32)
    for ref, part in ((send_ref, product[:rows]), (keep_ref, product[rows:])):
        ref[:, base:] = jnp.zeros((rows, 2 * lane), F32)
        ref[:, base : base + comps] = part
        ref[:, base + lane : base + lane + comps] = w


def encode_kernel(where_ref, keep_ref, got_ref, out_ref, partner_ref):
    lane = LANE
    chunks, rows, width = out_ref.shape
    base = width - 2 * lane
    comps = partner_ref.shape[1]
    tile = keep_ref.shape[0]
    y, core = where_ref[3], where_ref[2]
    at_first = core == 0
    mine = keep_ref[:, base + lane :]
    other = got_ref[:, base + lane :]
    bottom = jnp.where(at_first, other[tile - 8 :], mine[tile - 8 :])
    top = jnp.where(at_first, mine[:8], other[:8])
    partner_ref[...] = jnp.where(at_first, other[:8], other[tile - 8 :])[:, :comps]
    for i in range(chunks):
        at = slice(i * rows, (i + 1) * rows)
        for j in range(base // lane):
            block = slice(j * lane, (j + 1) * lane)
            out_ref[i, :, block] = encode(keep_ref[at, block] + got_ref[at, block])
        block = slice(base, base + lane)
        out_ref[i, :, block] = encode((keep_ref[at, block] + got_ref[at, block]) * GRAM_SCALE)
        rim = jnp.where(i == y + 1, bottom, jnp.where(i == y - 1, top, 0.0))
        scaled = rim * 32768.0
        coarse = scaled.astype(jnp.int32)
        fine = ((scaled - coarse.astype(F32)) * 65536.0).astype(jnp.int32)
        both = jnp.where(iota((rows, lane), 1) < comps, coarse, pltpu.roll(fine, comps, 1))
        out_ref[i, :, base + lane :] = (both - OFFSET).astype(jnp.int16)


def merge_kernel(where_ref, codes_ref, partner_ref, w_ref, out_ref, rim_ref):
    lane = LANE
    chunks, rows, width = codes_ref.shape
    base = width - 2 * lane
    tile, comps = w_ref.shape
    y, core = where_ref[3], where_ref[2]

    def total(block):
        out = decode(codes_ref[0, :, block])
        for i in range(1, chunks):
            out = out + decode(codes_ref[i, :, block])
        return out

    for j in range(base // lane):
        block = slice(j * lane, (j + 1) * lane)
        out_ref[:, block] = total(block)
    out_ref[:, base : base + lane] = total(slice(base, base + lane)) * (1.0 / GRAM_SCALE)

    pair = jnp.concatenate([w_ref[...], w_ref[...]], axis=1)
    first = iota((8, lane), 1) < comps
    heads = jnp.concatenate([pair[8 * i : 8 * i + 1] for i in range(8)], axis=0)
    tails = jnp.concatenate([pair[8 * i + 7 : 8 * i + 8] for i in range(8)], axis=0)
    out_ref[:, base + lane :] = jnp.where(first, heads, tails)

    source = jnp.where(core == 0, y - 1, y + 1)
    inside = jnp.logical_and(source >= 0, source < chunks)
    both = codes_ref[jnp.clip(source, 0, chunks - 1), :, base + lane :].astype(jnp.int32) + OFFSET
    both = both.astype(F32)
    outer = both * (1.0 / 32768.0) + pltpu.roll(both, comps, 1) * (1.0 / 2147483648.0)
    outer = jnp.where(inside, outer, 0.0)[:, :comps]
    partner = partner_ref[...]
    rim_ref[0] = jnp.where(core == 0, outer, partner)
    rim_ref[1] = jnp.where(core == 0, partner, outer)


def spectra_kernel(tv_strength, where_ref, parts_ref, rim_ref, comps_ref, w_ref, h_low_ref, h_ref, tv_num_ref, tv_den_ref):
    lane = LANE
    half_blocks = h_low_ref.shape[1] // lane
    base = half_blocks * lane
    comps = comps_ref.shape[0]
    me, side = where_ref[0], where_ref[1]
    sides = parts_ref.shape[0]

    def total(start):
        block = parts_ref[0, :, pl.ds(start, lane)]
        for i in range(1, sides):
            block = block + parts_ref[i, :, pl.ds(start, lane)]
        return block

    gram = jnp.transpose(total(base))[:comps, :]
    weights = [jnp.broadcast_to(gram[:, i : i + 1], (comps, lane)) for i in range(4)]
    odd = me % 2
    own_at = pl.ds(pl.multiple_of(8 * (me // 2), 8), 8)
    top = iota((8, lane), 0) < 4

    def block_step(j, carry):
        numer = total(pl.multiple_of(j * lane, lane))
        denominators = []
        own = []
        for half in range(2):
            at = pl.ds(pl.multiple_of((half * half_blocks + j) * lane, lane), lane)
            block = comps_ref[:, at]
            for i in range(4):
                denominators.append(jnp.sum(block * weights[i], axis=0, keepdims=True))
            own.append(comps_ref[own_at, at])
        denominator = jnp.concatenate(denominators, axis=0)
        own_rows = jnp.where(top, pltpu.roll(own[0], 4 * odd, 0), pltpu.roll(own[1], 4 * (1 - odd), 0))
        h = own_rows * numer / denominator
        h_low_ref[:, pl.ds(pl.multiple_of(j * lane, lane), lane)] = h.astype(BF16)
        turned = pltpu.roll(h, lax.rem(8 - side, 8), 0)
        h_ref[:, pl.ds(pl.multiple_of(j * lane, lane), lane)] = turned[0:1]
        h_ref[:, pl.ds(pl.multiple_of((half_blocks + j) * lane, lane), lane)] = turned[4:5]
        return carry

    lax.fori_loop(0, half_blocks, block_step, 0)

    above, below = rim_ref[0], rim_ref[1]
    before = parts_ref[jnp.maximum(side - 1, 0), :, base + lane :][:, comps:]
    before = jnp.where(side > 0, before, 0.0)
    after = parts_ref[jnp.minimum(side + 1, sides - 1), :, base + lane :][:, :comps]
    after = jnp.where(side < sides - 1, after, 0.0)
    spot = iota((8, comps), 0)
    rows = [w_ref[8 * i : 8 * i + 8, :] for i in range(8)]
    for i in range(8):
        centre = rows[i]
        beside = (
            rows[i + 1] if i < 7 else below,
            rows[i - 1] if i > 0 else above,
            jnp.where(spot == 7, after[i : i + 1], pltpu.roll(centre, 7, 0)),
            jnp.where(spot == 0, before[i : i + 1], pltpu.roll(centre, 1, 0)),
        )
        num = jnp.zeros_like(centre)
        den = jnp.zeros_like(centre)
        for q in beside:
            edge_weight = 1.0 / (jnp.abs(centre - q) + tv_edge)
            num = num + edge_weight * q
            den = den + edge_weight * centre
        tv_num_ref[8 * i : 8 * i + 8, :] = tv_strength * num
        tv_den_ref[8 * i : 8 * i + 8, :] = tv_strength * den


def project_kernel(where_ref, mine_ref, other_ref, dense_ref, out_ref):
    half_blocks, two_tiles, lane = dense_ref.shape
    comps = mine_ref.shape[0]
    rows = 2 * comps
    copies, tile, _ = out_ref.shape
    core = where_ref[2]
    cross = jnp.zeros((two_tiles, rows), F32)
    spec = jnp.zeros((rows, rows), F32)
    for j in range(half_blocks):
        at = slice(j * lane, (j + 1) * lane)
        block = jnp.concatenate([mine_ref[:, at], other_ref[:, at]], axis=0)
        cross = cross + nt(dense_ref[j], block)
        spec = spec + nt(block, block)
    row, col = iota((two_tiles, rows), 0), iota((two_tiles, rows), 1)
    cross = jnp.where(row // tile == (col // 4) % 2, cross, 0.0)
    cross = cross[:tile] + cross[tile:]
    row, col = iota((rows, rows), 0), iota((rows, rows), 1)
    spec = jnp.where((row // 4) % 2 == (col // 4) % 2, spec, 0.0)
    row_core = jnp.where(row < comps, core, 1 - core)
    name = 8 * (row % comps // 8) + 4 * row_core + row % 4
    to_low = jnp.where(col == name, 1.0, 0.0)
    to_high = jnp.where(iota((comps, rows), 1) == iota((comps, rows), 0) + comps, 1.0, 0.0)
    exact = dict(preferred_element_type=F32, precision=lax.Precision.HIGHEST)
    spec = lax.dot_general(to_low, spec, (((0,), (0,)), ((), ())), **exact)[:comps]
    spec = jnp.dot(spec, to_low, **exact)[:, :comps]
    both = jnp.dot(cross, to_low, **exact) + jnp.dot(spec, to_high, **exact)
    for i in range(copies):
        out_ref[i] = both


def sum_kernel(parts_ref, out_ref):
    block = parts_ref[0]
    for i in range(1, parts_ref.shape[0]):
        block = block + parts_ref[i]
    out_ref[...] = block


def loadings_kernel(parts_ref, w_ref, tv_num_ref, tv_den_ref, out_ref):
    comps = w_ref.shape[1]
    block = parts_ref[0]
    for i in range(1, parts_ref.shape[0]):
        block = block + parts_ref[i]
    w = w_ref[...]
    fitted = jnp.dot(w, block, preferred_element_type=F32, precision=lax.Precision.HIGHEST)
    fitted = pltpu.roll(fitted, comps, 1)[:, :comps]
    out_ref[...] = w * (block[:, :comps] + tv_num_ref[...]) / (fitted + tv_den_ref[...])


def local(spectra, block_ids, counts, loadings, components):
    tile_x, tile_y, slot_count, lane = spectra.shape
    tile = tile_x * tile_y
    comps = loadings.shape[2]
    slab_bins = components.shape[1]
    half_blocks = slab_bins // lane // 2
    half_bins = half_blocks * lane
    width = half_bins + 2 * lane
    spots = [lax.axis_index(axis) for axis in (("y", "core"), "gy", "core", "y")]
    here = jnp.stack(spots).astype(jnp.int32)
    chunks = lax.axis_size("y")
    pixels = spectra.transpose(0, 2, 1, 3)
    w = loadings.reshape(tile, comps)
    swap = [(0, 1), (1, 0)]

    send, keep, dense = pl.pallas_call(
        numer_kernel,
        out_shape=(
            jax.ShapeDtypeStruct((comps, width), F32),
            jax.ShapeDtypeStruct((comps, width), F32),
            jax.ShapeDtypeStruct((half_blocks, 2 * tile, lane), BF16),
        ),
        in_specs=[smem(), smem(), smem(), vmem(), vmem()],
        out_specs=(vmem(),) * 3,
        compiler_params=params(),
        name="numer",
    )(here, block_ids.reshape(slot_count), counts.reshape(1), pixels, w)
    got = lax.ppermute(send, "core", swap)
    codes, partner = pl.pallas_call(
        encode_kernel,
        out_shape=(
            jax.ShapeDtypeStruct((chunks, 8, width), jnp.int16),
            jax.ShapeDtypeStruct((8, comps), F32),
        ),
        in_specs=[smem(), vmem(), vmem()],
        out_specs=(vmem(),) * 2,
        compiler_params=params(),
        name="encode",
    )(here, keep, got)
    codes = lax.all_to_all(codes, "y", 0, 0, tiled=True)
    merged, rims = pl.pallas_call(
        merge_kernel,
        out_shape=(
            jax.ShapeDtypeStruct((8, width), F32),
            jax.ShapeDtypeStruct((2, 8, comps), F32),
        ),
        in_specs=[smem(), vmem(), vmem(), vmem()],
        out_specs=(vmem(),) * 2,
        compiler_params=params(),
        name="merge",
    )(here, codes, partner, w)
    parts = lax.all_gather(merged, "gy", axis=0)

    tv_strength = tv_share * slab_bins * lax.axis_size(("w", "x"))
    h_low, h_next, tv_num, tv_den = pl.pallas_call(
        functools.partial(spectra_kernel, tv_strength),
        out_shape=(
            jax.ShapeDtypeStruct((8, half_bins), BF16),
            jax.ShapeDtypeStruct((1, slab_bins), F32),
            jax.ShapeDtypeStruct((tile, comps), F32),
            jax.ShapeDtypeStruct((tile, comps), F32),
        ),
        in_specs=[smem(), vmem(), vmem(), vmem(), vmem()],
        out_specs=(vmem(),) * 4,
        compiler_params=params(),
        name="spectra",
    )(here, parts, rims, components, w)

    h_mine = lax.all_gather(h_low, "y", axis=0, tiled=True)
    h_other = lax.ppermute(h_mine, "core", swap)

    copies = lax.axis_size("x")
    both = pl.pallas_call(
        project_kernel,
        out_shape=jax.ShapeDtypeStruct((copies, tile, 2 * comps), F32),
        in_specs=[smem(), vmem(), vmem(), vmem()],
        out_specs=vmem(),
        compiler_params=params(),
        name="project",
    )(here, h_mine, h_other, dense)

    both = lax.all_to_all(both, "x", 0, 0, tiled=True)
    both = pl.pallas_call(
        sum_kernel,
        out_shape=jax.ShapeDtypeStruct((tile, 2 * comps), F32),
        in_specs=[vmem()],
        out_specs=vmem(),
        compiler_params=params(),
        name="sum",
    )(both)
    both = lax.all_gather(both, "w", axis=0)
    w_next = pl.pallas_call(
        loadings_kernel,
        out_shape=jax.ShapeDtypeStruct((tile, comps), F32),
        in_specs=[vmem()] * 4,
        out_specs=vmem(),
        compiler_params=params(),
        name="loadings",
    )(both, w, tv_num, tv_den)
    return (w_next.reshape(tile_x, tile_y, comps), h_next)


def solution(mesh):
    gx, gy, mz = mesh.devices.shape
    fine = Mesh(mesh.devices.reshape(gx // 2, 2, gy, 4, mz // 4), ("y", "core", "gy", "w", "x"))
    rows, slabs = ("y", "core"), ("w", "x")
    in_specs = (
        P(rows, "gy", slabs, None),
        P(rows, "gy", slabs),
        P(rows, "gy", slabs),
        P(rows, "gy", None),
        P(None, slabs),
    )
    out_specs = (P(rows, "gy", None), P(("y", "core", "gy"), slabs))
    return jax.shard_map(local, mesh=fine, in_specs=in_specs, out_specs=out_specs, check_vma=False)
```

```python
import functools
import jax
import jax.numpy as jnp
from jax import lax
from jax.experimental import pallas as pl
from jax.experimental.pallas import tpu as pltpu
from jax.sharding import Mesh, PartitionSpec as P

tv_edge = 0.1
tv_share = 0.1
LANE = 128
VMEM_LIMIT = 48 * 1024 * 1024
F32 = jnp.float32
BF16 = jnp.bfloat16


def params():
    return pltpu.CompilerParams(vmem_limit_bytes=VMEM_LIMIT)


def vmem():
    return pl.BlockSpec(memory_space=pltpu.VMEM)


def smem():
    return pl.BlockSpec(memory_space=pltpu.SMEM)


def iota(shape, dim):
    return lax.broadcasted_iota(jnp.int32, shape, dim)


def nt(a, b):
    return lax.dot_general(a, b, (((1,), (1,)), ((), ())), preferred_element_type=F32)


LOG_LOW = 3.25
LOG_STEPS = 5950.0
GRAM_SCALE = 64.0
OFFSET = 32768


def encode(value):
    steps = (jnp.log2(jnp.maximum(value, 1.0)) - LOG_LOW) * LOG_STEPS
    code = jnp.where(value > 0.0, jnp.maximum(steps, 0.0) + 1.5, 0.0).astype(jnp.int32)
    return jnp.minimum(code, 65535)


def decode(code):
    steps = code.astype(jnp.int32).astype(F32) + float(OFFSET)
    return jnp.where(steps > 0.0, jnp.exp2((steps - 1.0) * (1.0 / LOG_STEPS) + LOG_LOW), 0.0)


GRAM_ROW = 14
HALO_ROW = 15


def numer_kernel(where_ref, ids_ref, count_ref, x_ref, w_ref, send_ref, keep_ref, dense_ref):
    tile_x, slots, tile_y, lane = x_ref.shape
    tile = tile_x * tile_y
    blocks = dense_ref.shape[0]
    comps = w_ref.shape[1]
    half = comps // 2
    across = keep_ref.shape[0]
    depth = keep_ref.shape[1] // half
    core = where_ref[2]

    w = w_ref[...]
    w_low = w.astype(BF16)
    row = iota((comps, comps), 0)
    name = 8 * (row % half // 4) + 4 * jnp.where(row < half, 1 - core, core) + row % 4
    pick = jnp.where(iota((comps, comps), 1) == name, 1.0, 0.0).astype(BF16)
    left = nt(pick, w_low).astype(BF16)

    dense_ref[...] = jnp.zeros_like(dense_ref)

    def place(s, carry):
        dense_ref[ids_ref[s]] = x_ref[:, s].astype(F32).reshape(tile, lane).astype(BF16)
        return carry

    lax.fori_loop(0, count_ref[0], place, 0)

    def put(ref, r, j, value):
        ref[j, pl.ds(r, half, stride=depth), :] = value

    for b in range(0, blocks, 2):
        right = jnp.concatenate([dense_ref[b], dense_ref[b + 1]], axis=1)
        product = jnp.dot(left, right, preferred_element_type=F32)
        for i in range(2):
            r, j = divmod(b + i, across)
            put(send_ref, r, j, product[:half, i * lane : (i + 1) * lane])
            put(keep_ref, r, j, product[half:, i * lane : (i + 1) * lane])

    product = jnp.dot(left, jnp.concatenate([w_low, w_low], axis=1), preferred_element_type=F32)
    wide = jnp.concatenate([w[:half], w[half:]], axis=1)
    empty = jnp.zeros((half, lane), F32)
    for ref, part in ((send_ref, product[:half]), (keep_ref, product[half:])):
        for j in range(across):
            put(ref, GRAM_ROW, j, part if j == 0 else wide if j == 1 else empty)
            put(ref, HALO_ROW, j, empty)


def rim_codes(rim):
    scaled = jnp.concatenate([rim, rim], axis=1) * 32768.0
    coarse = scaled.astype(jnp.int32)
    fine = ((scaled - coarse.astype(F32)) * 65536.0).astype(jnp.int32)
    return jnp.where(iota(scaled.shape, 1) < rim.shape[1], coarse, fine)


def encode_kernel(where_ref, keep_ref, got_ref, w_ref, out_ref, partner_ref):
    lane = LANE
    chunks, depth, width = out_ref.shape
    sides = 4
    tile, comps = w_ref.shape
    half = comps // 2
    side, core, y = where_ref[1], where_ref[2], where_ref[3]
    at_first = core == 0
    w = w_ref[...]
    wide = got_ref[1, pl.ds(GRAM_ROW, half, stride=depth), :]
    partner_top, partner_bottom = wide[:8, :comps], wide[half - 8 :, comps:]
    partner_ref[...] = jnp.where(at_first, partner_top, partner_bottom)
    bottom = rim_codes(jnp.where(at_first, partner_bottom, w[tile - 8 :]))
    top = rim_codes(jnp.where(at_first, w[:8], partner_top))
    first = rim_codes(jnp.concatenate([w[8 * i : 8 * i + 1] for i in range(8)], axis=0))
    last = rim_codes(jnp.concatenate([w[8 * i + 7 : 8 * i + 8] for i in range(8)], axis=0))
    row = iota((depth, lane), 0)
    scale = jnp.where(row == GRAM_ROW, GRAM_SCALE, 1.0)
    for i in range(chunks):
        to_y, to_side = divmod(i, sides)
        same_side, same_y = side == to_side, y == to_y
        halo = jnp.where(jnp.logical_and(same_side, y + 1 == to_y), bottom, 0)
        halo = jnp.where(jnp.logical_and(same_side, y - 1 == to_y), top, halo)
        halo = jnp.where(jnp.logical_and(same_y, side + 1 == to_side), last, halo)
        halo = jnp.where(jnp.logical_and(same_y, side - 1 == to_side), first, halo)
        at = slice(i * depth, (i + 1) * depth)
        for j in range(width // lane):
            block = slice(j * lane, (j + 1) * lane)
            value = keep_ref[j, at, :] + got_ref[j, at, :]
            code = encode(value * scale if j == 0 else value)
            code = jnp.where(row == HALO_ROW, halo[j : j + 1], code)
            if j == 1:
                code = jnp.where(row == GRAM_ROW, halo[7:8], code)
            out_ref[i, :, block] = (code - OFFSET).astype(jnp.int16)


def spectra_kernel(tv_strength, where_ref, codes_ref, partner_ref, comps_ref, w_ref, h_all_ref, h_ref, tv_num_ref, tv_den_ref):
    lane = LANE
    chunks, depth, width = codes_ref.shape
    across = width // lane
    sides = 4
    tile, comps = w_ref.shape
    side, core, y = where_ref[1], where_ref[2], where_ref[3]
    turn = lax.rem(8 - 4 * core - side, 8)

    def total(j):
        block = slice(j * lane, (j + 1) * lane)
        out = decode(codes_ref[0, :, block])
        for i in range(1, chunks):
            out = out + decode(codes_ref[i, :, block])
        return out

    sums = [total(j) for j in range(across)]
    gram = jnp.transpose(sums[0])[:comps, GRAM_ROW : GRAM_ROW + 1] * (1.0 / GRAM_SCALE)
    gram = jnp.broadcast_to(gram, (comps, lane))
    for j in range(across):
        denominators, own_rows = [], []
        for r in range(GRAM_ROW):
            block = slice((r * across + j) * lane, (r * across + j + 1) * lane)
            denominators.append(jnp.sum(comps_ref[:, block] * gram, axis=0, keepdims=True))
            group = comps_ref[pl.ds(pl.multiple_of(8 * y, 8), 8), block]
            own_rows.append(pltpu.roll(group, turn, 0)[:1])
        denominators.append(jnp.ones((depth - GRAM_ROW, lane), F32))
        own_rows.append(jnp.zeros((depth - GRAM_ROW, lane), F32))
        h = jnp.concatenate(own_rows, axis=0) * sums[j] / jnp.concatenate(denominators, axis=0)
        for r in range(GRAM_ROW):
            h_ref[:, (r * across + j) * lane : (r * across + j + 1) * lane] = h[r : r + 1]
        h_low = h.astype(BF16)
        for i in range(chunks):
            h_all_ref[i, :, j * lane : (j + 1) * lane] = h_low

    def halo(from_y, from_side):
        inside = jnp.logical_and(
            jnp.logical_and(from_y >= 0, from_y < chunks // sides), jnp.logical_and(from_side >= 0, from_side < sides)
        )
        source = jnp.where(inside, from_y * sides + from_side, 0)
        rows = [
            codes_ref[source, :, j * lane : (j + 1) * lane].astype(jnp.int32)[HALO_ROW : HALO_ROW + 1]
            for j in range(across)
        ]
        rows.append(codes_ref[source, :, lane : 2 * lane].astype(jnp.int32)[GRAM_ROW : GRAM_ROW + 1])
        both = (jnp.concatenate(rows, axis=0) + OFFSET).astype(F32)
        value = both * (1.0 / 32768.0) + pltpu.roll(both, comps, 1) * (1.0 / 2147483648.0)
        return jnp.where(inside, value, 0.0)[:, :comps]

    outer = halo(jnp.where(core == 0, y - 1, y + 1), side)
    before, after = halo(y, side - 1), halo(y, side + 1)
    partner = partner_ref[...]
    above = jnp.where(core == 0, outer, partner)
    below = jnp.where(core == 0, partner, outer)
    spot = iota((8, comps), 0)
    rows = [w_ref[8 * i : 8 * i + 8, :] for i in range(8)]
    for i in range(8):
        centre = rows[i]
        beside = (
            rows[i + 1] if i < 7 else below,
            rows[i - 1] if i > 0 else above,
            jnp.where(spot == 7, after[i : i + 1], pltpu.roll(centre, 7, 0)),
            jnp.where(spot == 0, before[i : i + 1], pltpu.roll(centre, 1, 0)),
        )
        num = jnp.zeros_like(centre)
        den = jnp.zeros_like(centre)
        for q in beside:
            edge_weight = 1.0 / (jnp.abs(centre - q) + tv_edge)
            num = num + edge_weight * q
            den = den + edge_weight * centre
        tv_num_ref[8 * i : 8 * i + 8, :] = tv_strength * num
        tv_den_ref[8 * i : 8 * i + 8, :] = tv_strength * den


def project_kernel(where_ref, mine_ref, other_ref, dense_ref, out_ref, wide_ref):
    blocks, tile, lane = dense_ref.shape
    half, depth, width = mine_ref.shape
    across = width // lane
    comps = 2 * half
    copies = out_ref.shape[0]
    core = where_ref[2]
    for i, ref in enumerate((mine_ref, other_ref)):
        for j in range(across):
            block = ref[:, :, j * lane : (j + 1) * lane]
            wide_ref[i, j] = block.astype(F32).reshape(half * depth, lane)

    def spectrum(b):
        r, j = divmod(b, across)
        parts = [wide_ref[i, j, pl.ds(r, half, stride=depth), :] for i in range(2)]
        return jnp.concatenate(parts, axis=0).astype(BF16)

    total = jnp.zeros((tile + comps, comps), F32)
    for b in range(0, blocks, 2):
        h = jnp.concatenate([spectrum(b), spectrum(b + 1)], axis=1)
        x = jnp.concatenate([dense_ref[b], dense_ref[b + 1]], axis=1)
        total = total + nt(jnp.concatenate([x, h], axis=0), h)
    row = iota((comps, lane), 0)
    name = 8 * (row % half // 4) + 4 * jnp.where(row < half, core, 1 - core) + row % 4
    to_low = jnp.where(iota((comps, lane), 1) == name, 1.0, 0.0)
    to_high = jnp.where(iota((comps, lane), 1) == name + comps, 1.0, 0.0)
    exact = dict(preferred_element_type=F32, precision=lax.Precision.HIGHEST)
    spec = lax.dot_general(to_low, total[tile:], (((0,), (0,)), ((), ())), **exact)[:comps]
    both = jnp.dot(total[:tile], to_low, **exact) + jnp.dot(spec, to_high, **exact)
    for i in range(copies):
        out_ref[i] = both


def sum_kernel(parts_ref, out_ref):
    block = parts_ref[0]
    for i in range(1, parts_ref.shape[0]):
        block = block + parts_ref[i]
    out_ref[...] = block


def loadings_kernel(parts_ref, w_ref, tv_num_ref, tv_den_ref, out_ref):
    comps = w_ref.shape[1]
    block = parts_ref[0]
    for i in range(1, parts_ref.shape[0]):
        block = block + parts_ref[i]
    w = w_ref[...]
    fitted = jnp.dot(w, block, preferred_element_type=F32, precision=lax.Precision.HIGHEST)
    fitted = pltpu.roll(fitted, comps, 1)[:, :comps]
    out_ref[...] = w * (block[:, :comps] + tv_num_ref[...]) / (fitted + tv_den_ref[...])


def local(spectra, block_ids, counts, loadings, components):
    tile_x, tile_y, slot_count, lane = spectra.shape
    tile = tile_x * tile_y
    comps = loadings.shape[2]
    slab_bins = components.shape[1]
    blocks = slab_bins // lane
    half = comps // 2
    depth = 16
    width = slab_bins // GRAM_ROW
    spots = [lax.axis_index(axis) for axis in (("y", "core"), "gy", "core", "y")]
    here = jnp.stack(spots).astype(jnp.int32)
    peers = ("y", "gy")
    chunks = lax.axis_size(peers)
    pixels = spectra.transpose(0, 2, 1, 3)
    w = loadings.reshape(tile, comps)
    swap = [(0, 1), (1, 0)]

    send, keep, dense = pl.pallas_call(
        numer_kernel,
        out_shape=(
            jax.ShapeDtypeStruct((width // lane, half * depth, lane), F32),
            jax.ShapeDtypeStruct((width // lane, half * depth, lane), F32),
            jax.ShapeDtypeStruct((blocks, tile, lane), BF16),
        ),
        in_specs=[smem(), smem(), smem(), vmem(), vmem()],
        out_specs=(vmem(),) * 3,
        compiler_params=params(),
        name="numer",
    )(here, block_ids.reshape(slot_count), counts.reshape(1), pixels, w)
    got = lax.ppermute(send, "core", swap)
    codes, partner = pl.pallas_call(
        encode_kernel,
        out_shape=(
            jax.ShapeDtypeStruct((chunks, depth, width), jnp.int16),
            jax.ShapeDtypeStruct((8, comps), F32),
        ),
        in_specs=[smem(), vmem(), vmem(), vmem()],
        out_specs=(vmem(),) * 2,
        compiler_params=params(),
        name="encode",
    )(here, keep, got, w)
    codes = lax.all_to_all(codes, peers, 0, 0, tiled=True)
    tv_strength = tv_share * slab_bins * lax.axis_size(("w", "x"))
    h_all, h_next, tv_num, tv_den = pl.pallas_call(
        functools.partial(spectra_kernel, tv_strength),
        out_shape=(
            jax.ShapeDtypeStruct((chunks, depth, width), BF16),
            jax.ShapeDtypeStruct((1, slab_bins), F32),
            jax.ShapeDtypeStruct((tile, comps), F32),
            jax.ShapeDtypeStruct((tile, comps), F32),
        ),
        in_specs=[smem(), vmem(), vmem(), vmem(), vmem()],
        out_specs=(vmem(),) * 4,
        compiler_params=params(),
        name="spectra",
    )(here, codes, partner, components, w)

    h_mine = lax.all_to_all(h_all, peers, 0, 0, tiled=True)
    h_other = lax.ppermute(h_mine, "core", swap)

    copies = lax.axis_size("x")
    both = pl.pallas_call(
        project_kernel,
        out_shape=jax.ShapeDtypeStruct((copies, tile, 2 * comps), F32),
        in_specs=[smem(), vmem(), vmem(), vmem()],
        out_specs=vmem(),
        scratch_shapes=[pltpu.VMEM((2, width // lane, half * depth, lane), F32)],
        compiler_params=params(),
        name="project",
    )(here, h_mine, h_other, dense)

    both = lax.all_to_all(both, "x", 0, 0, tiled=True)
    both = pl.pallas_call(
        sum_kernel,
        out_shape=jax.ShapeDtypeStruct((tile, 2 * comps), F32),
        in_specs=[vmem()],
        out_specs=vmem(),
        compiler_params=params(),
        name="sum",
    )(both)
    both = lax.all_gather(both, "w", axis=0)
    w_next = pl.pallas_call(
        loadings_kernel,
        out_shape=jax.ShapeDtypeStruct((tile, comps), F32),
        in_specs=[vmem()] * 4,
        out_specs=vmem(),
        compiler_params=params(),
        name="loadings",
    )(both, w, tv_num, tv_den)
    return (w_next.reshape(tile_x, tile_y, comps), h_next)


def solution(mesh):
    gx, gy, mz = mesh.devices.shape
    fine = Mesh(mesh.devices.reshape(gx // 2, 2, gy, 4, mz // 4), ("y", "core", "gy", "w", "x"))
    rows, slabs = ("y", "core"), ("w", "x")
    in_specs = (
        P(rows, "gy", slabs, None),
        P(rows, "gy", slabs),
        P(rows, "gy", slabs),
        P(rows, "gy", None),
        P(None, slabs),
    )
    out_specs = (P(rows, "gy", None), P(("y", "core", "gy"), slabs))
    return jax.shard_map(local, mesh=fine, in_specs=in_specs, out_specs=out_specs, check_vma=False)
```

```python
import functools
import jax
import jax.numpy as jnp
from jax import lax
from jax.experimental import pallas as pl
from jax.experimental.pallas import tpu as pltpu
from jax.sharding import Mesh, PartitionSpec as P

tv_edge = 0.1
tv_share = 0.1
LANE = 128
VMEM_LIMIT = 48 * 1024 * 1024
F32 = jnp.float32
BF16 = jnp.bfloat16


def params():
    return pltpu.CompilerParams(vmem_limit_bytes=VMEM_LIMIT)


def vmem():
    return pl.BlockSpec(memory_space=pltpu.VMEM)


def smem():
    return pl.BlockSpec(memory_space=pltpu.SMEM)


def iota(shape, dim):
    return lax.broadcasted_iota(jnp.int32, shape, dim)


def nt(a, b):
    return lax.dot_general(a, b, (((1,), (1,)), ((), ())), preferred_element_type=F32)


LOG_LOW = 3.25
LOG_STEPS = 5950.0
GRAM_SCALE = 64.0
OFFSET = 32768


def encode(value):
    steps = (jnp.log2(jnp.maximum(value, 1.0)) - LOG_LOW) * LOG_STEPS
    code = jnp.where(value > 0.0, jnp.maximum(steps, 0.0) + 1.5, 0.0).astype(jnp.int32)
    return jnp.minimum(code, 65535)


def decode(code):
    steps = code.astype(jnp.int32).astype(F32) + float(OFFSET)
    return jnp.where(steps > 0.0, jnp.exp2((steps - 1.0) * (1.0 / LOG_STEPS) + LOG_LOW), 0.0)


ACROSS = 13
DEPTH = 8
HALO = 4


def place_of(q):
    return divmod(q, ACROSS)


def component_of(row):
    return 8 * (row % 32 // 4) + 4 * (row // 32) + row % 4


def anywhere():
    return pl.BlockSpec(memory_space=pl.ANY)


def scatter_kernel(where_ref, ids_hbm, count_hbm, x_ref, w_ref, keep_ref, send_ref, ids_ref, count_ref, sems):
    copies = [
        pltpu.make_async_copy(ids_hbm, ids_ref, sems.at[0]),
        pltpu.make_async_copy(count_hbm, count_ref, sems.at[1]),
    ]
    for copy in copies:
        copy.start()
    tile_x, slots, tile_y, lane = x_ref.shape
    tile, comps = w_ref.shape
    half_blocks = keep_ref.shape[0]
    core = where_ref[2]
    keep_ref[...] = jnp.zeros_like(keep_ref)
    send_ref[...] = jnp.zeros_like(send_ref)
    w = w_ref[...]
    edges = jnp.concatenate([w[:8], w[tile - 8 :]], axis=0)
    high = edges.astype(BF16).astype(F32)
    mid = (edges - high).astype(BF16).astype(F32)
    pieces = jnp.concatenate([high, mid, edges - high - mid, jnp.zeros_like(edges)], axis=0)
    send_ref[half_blocks] = jnp.concatenate([w, pieces], axis=1).astype(BF16)
    for copy in copies:
        copy.wait()

    def place(s, carry):
        block = ids_ref[s]
        high = block // half_blocks
        at = block - high * half_blocks
        rows_of_slot = x_ref[:, s].astype(F32).reshape(tile, lane).astype(BF16)

        @pl.when(high == core)
        def _():
            keep_ref[at] = rows_of_slot

        @pl.when(high != core)
        def _():
            send_ref[at] = rows_of_slot

        return carry

    lax.fori_loop(0, count_ref[0], place, 0)


def rims(where_ref, w, edges):
    at_first = where_ref[2] == 0
    tile = w.shape[0]
    bottom = jnp.where(at_first, edges[8:], w[tile - 8 :])
    top = jnp.where(at_first, w[:8], edges[:8])
    first = jnp.concatenate([w[8 * i : 8 * i + 1] for i in range(8)], axis=0)
    last = jnp.concatenate([w[8 * i + 7 : 8 * i + 8] for i in range(8)], axis=0)
    return [jnp.concatenate([rim[:4], rim[4:]], axis=1) for rim in (bottom, top, last, first)]


def coarse_part(value):
    return (value * 32768.0 + 0.5).astype(jnp.int32)


def rim_for(i, where_ref, values):
    side, y = where_ref[1], where_ref[3]
    to_y, to_side = divmod(i, 4)
    same_side, same_y = side == to_side, y == to_y
    out = jnp.where(jnp.logical_and(same_side, y + 1 == to_y), values[0], jnp.zeros_like(values[0]))
    out = jnp.where(jnp.logical_and(same_side, y - 1 == to_y), values[1], out)
    out = jnp.where(jnp.logical_and(same_y, side + 1 == to_side), values[2], out)
    return jnp.where(jnp.logical_and(same_y, side - 1 == to_side), values[3], out)


def rim_sources(where_ref, chunks):
    side, core, y = where_ref[1], where_ref[2], where_ref[3]
    out = []
    for from_y, from_side in ((jnp.where(core == 0, y - 1, y + 1), side), (y, side - 1), (y, side + 1)):
        inside = jnp.logical_and(
            jnp.logical_and(from_y >= 0, from_y < chunks // 4), jnp.logical_and(from_side >= 0, from_side < 4)
        )
        out.append((jnp.where(inside, from_y * 4 + from_side, 0), inside))
    return out


def unfold(rows):
    half = rows.shape[1] // 2
    return jnp.concatenate([rows[:, :half], rows[:, half:]], axis=0)


def numer_kernel(where_ref, keep_ref, got_ref, w_ref, codes_ref, edges_ref, wide_ref):
    half_blocks, tile, lane = keep_ref.shape
    comps = w_ref.shape[1]
    chunks = codes_ref.shape[0]
    w = w_ref[...]
    apart = got_ref[half_blocks]
    pieces = apart[:, comps:].astype(F32)
    edges = pieces[:16] + pieces[16:32] + pieces[32:48]
    edges_ref[...] = edges
    w_two = jnp.concatenate([w.astype(BF16), apart[:, :comps]], axis=0)
    pick = jnp.where(iota((comps, comps), 1) == component_of(iota((comps, comps), 0)), 1.0, 0.0).astype(BF16)
    left = nt(pick, w_two).astype(BF16)

    def put(q, value):
        r, j = place_of(q)
        wide_ref[j, pl.ds(r, chunks, stride=DEPTH), :] = value

    def both_tiles(b):
        return jnp.concatenate([keep_ref[b], got_ref[b]], axis=0)

    for b in range(0, half_blocks, 2):
        group = range(b, min(b + 2, half_blocks))
        right = jnp.concatenate([both_tiles(i) for i in group], axis=1)
        product = jnp.dot(left, right, preferred_element_type=F32)
        for i in group:
            for m in range(2):
                put(m * half_blocks + i, product[m * chunks : (m + 1) * chunks, (i - b) * lane : (i - b + 1) * lane])
    gram = jnp.dot(left, w_two, preferred_element_type=F32) * GRAM_SCALE
    put(2 * half_blocks, jnp.concatenate([gram[:chunks], gram[chunks:]], axis=1))
    for q in range(2 * half_blocks + 1, ACROSS * DEPTH):
        put(q, jnp.zeros((chunks, lane), F32))

    rim_values = [coarse_part(rim) for rim in rims(where_ref, w, edges)]
    row = iota((DEPTH, lane), 0)
    halo_row, halo_at = place_of(2 * half_blocks + 1)
    for i in range(chunks):
        rim = rim_for(i, where_ref, rim_values)
        for j in range(ACROSS):
            code = encode(wide_ref[j, i * DEPTH : (i + 1) * DEPTH, :])
            if halo_at <= j < halo_at + HALO:
                code = jnp.where(row == halo_row, rim[j - halo_at : j - halo_at + 1], code)
            codes_ref[i, :, j * lane : (j + 1) * lane] = (code - OFFSET).astype(jnp.int16)


def spectra_kernel(
    where_ref, codes_ref, edges_ref, comps_ref, w_ref, h_all_ref, mine_ref, send_ref, coarse_ref, first_ref, second_ref
):
    lane = LANE
    chunks = codes_ref.shape[0]
    tile, comps = w_ref.shape
    half_blocks = mine_ref.shape[1] // lane
    side, core, y = where_ref[1], where_ref[2], where_ref[3]
    turn = lax.rem(8 - side, 8)
    parts = (first_ref, second_ref)

    def total(j):
        block = slice(j * lane, (j + 1) * lane)
        out = decode(codes_ref[0, :, block])
        for i in range(1, chunks):
            out = out + decode(codes_ref[i, :, block])
        return out

    sums = [total(j) for j in range(ACROSS)]
    gram_row, gram_at = place_of(2 * half_blocks)
    gram = jnp.transpose(sums[gram_at])[:, gram_row : gram_row + 1] * (1.0 / GRAM_SCALE)
    grams = [jnp.broadcast_to(gram[m * comps : (m + 1) * comps], (comps, lane)) for m in range(2)]
    halo_row, halo_at = place_of(2 * half_blocks + 1)
    w = w_ref[...]
    rim_values = [rim - coarse_part(rim).astype(F32) * (1.0 / 32768.0) for rim in rims(where_ref, w, edges_ref[...])]
    rim_low = [rim_for(i, where_ref, rim_values) for i in range(chunks)]
    row = iota((DEPTH, lane), 0)
    for j in range(ACROSS):
        denominators, own_rows = [], []
        for r in range(DEPTH):
            q = r * ACROSS + j
            if q < 2 * half_blocks:
                m, b = divmod(q, half_blocks)
                at = pl.ds(pl.multiple_of((core * half_blocks + b) * lane, lane), lane)
                denominators.append(jnp.sum(comps_ref[:, at] * grams[m], axis=0, keepdims=True))
                group = comps_ref[pl.ds(pl.multiple_of(8 * y, 8), 8), at]
                own_rows.append(pltpu.roll(group, turn, 0)[4 * m : 4 * m + 1])
            else:
                denominators.append(jnp.ones((1, lane), F32))
                own_rows.append(jnp.zeros((1, lane), F32))
        h = jnp.concatenate(own_rows, axis=0) * sums[j] / jnp.concatenate(denominators, axis=0)
        for r in range(DEPTH):
            q = r * ACROSS + j
            if q < 2 * half_blocks:
                m, b = divmod(q, half_blocks)
                parts[m][:, b * lane : (b + 1) * lane] = h[r : r + 1]
        h_low = h.astype(BF16)
        for i in range(chunks):
            if halo_at <= j < halo_at + HALO:
                rim = rim_low[i][j - halo_at : j - halo_at + 1]
                h_low = jnp.where(row == halo_row, rim, h).astype(BF16)
            h_all_ref[i, :, j * lane : (j + 1) * lane] = h_low
    mine_ref[...] = jnp.where(core == 0, first_ref[...], second_ref[...])
    send_ref[...] = jnp.where(core == 0, second_ref[...], first_ref[...])

    for n, (source, inside) in enumerate(rim_sources(where_ref, chunks)):
        rows = [
            codes_ref[source, :, j * lane : (j + 1) * lane].astype(jnp.int32)[halo_row : halo_row + 1]
            for j in range(halo_at, halo_at + HALO)
        ]
        value = (jnp.concatenate(rows, axis=0) + OFFSET).astype(F32) * (1.0 / 32768.0)
        coarse_ref[8 * n : 8 * n + 8, :] = jnp.where(inside, unfold(value), 0.0)


def smooth(tv_strength, where_ref, outer, before, after, edges, w_ref, tv_num_ref, tv_den_ref):
    comps = w_ref.shape[1]
    at_first = where_ref[2] == 0
    above = jnp.where(at_first, outer, edges[8:])
    below = jnp.where(at_first, edges[:8], outer)
    spot = iota((8, comps), 0)
    rows = [w_ref[8 * i : 8 * i + 8, :] for i in range(8)]
    for i in range(8):
        centre = rows[i]
        beside = (
            rows[i + 1] if i < 7 else below,
            rows[i - 1] if i > 0 else above,
            jnp.where(spot == 7, after[i : i + 1], pltpu.roll(centre, 7, 0)),
            jnp.where(spot == 0, before[i : i + 1], pltpu.roll(centre, 1, 0)),
        )
        num = jnp.zeros_like(centre)
        den = jnp.zeros_like(centre)
        for q in beside:
            edge_weight = 1.0 / (jnp.abs(centre - q) + tv_edge)
            num = num + edge_weight * q
            den = den + edge_weight * centre
        tv_num_ref[8 * i : 8 * i + 8, :] = tv_strength * num
        tv_den_ref[8 * i : 8 * i + 8, :] = tv_strength * den


def project_kernel(
    tv_strength, where_ref, h_ref, keep_ref, got_ref, coarse_ref, edges_ref, w_ref, out_ref, tv_num_ref, tv_den_ref, wide_ref
):
    half_blocks, tile, lane = keep_ref.shape
    chunks = h_ref.shape[0]
    comps = w_ref.shape[1]
    copies = out_ref.shape[0]
    core = where_ref[2]
    for j in range(ACROSS):
        block = h_ref[:, :, j * lane : (j + 1) * lane]
        wide_ref[j] = block.astype(F32).reshape(chunks * DEPTH, lane)

    def spectrum(b):
        parts = []
        for m in range(2):
            r, j = place_of(m * half_blocks + b)
            parts.append(wide_ref[j, pl.ds(r, chunks, stride=DEPTH), :])
        return jnp.concatenate(parts, axis=0).astype(BF16)

    total = jnp.zeros((2 * tile + comps, comps), F32)
    for b in range(0, half_blocks, 2):
        group = range(b, min(b + 2, half_blocks))
        h = jnp.concatenate([spectrum(i) for i in group], axis=1)
        own = jnp.concatenate([keep_ref[i] for i in group], axis=1)
        partner = jnp.concatenate([got_ref[i] for i in group], axis=1)
        total = total + nt(jnp.concatenate([own, partner, h], axis=0), h)
    name = component_of(iota((comps, lane), 0))
    to_low = jnp.where(iota((comps, lane), 1) == name, 1.0, 0.0)
    to_high = jnp.where(iota((comps, lane), 1) == name + comps, 1.0, 0.0)
    exact = dict(preferred_element_type=F32, precision=lax.Precision.HIGHEST)
    spec = lax.dot_general(to_low, total[2 * tile :], (((0,), (0,)), ((), ())), **exact)[:comps]
    spec = jnp.dot(spec, to_high, **exact)
    cross = jnp.dot(total[: 2 * tile], to_low, **exact)
    for to_core in range(2):
        both = spec + jnp.where(core == to_core, cross[:tile], cross[tile:])
        for i in range(copies // 2):
            out_ref[to_core * (copies // 2) + i] = both

    halo_row, halo_at = place_of(2 * half_blocks + 1)
    halos = []
    for n, (source, inside) in enumerate(rim_sources(where_ref, chunks)):
        rows = [
            h_ref[source, :, j * lane : (j + 1) * lane].astype(F32)[halo_row : halo_row + 1]
            for j in range(halo_at, halo_at + HALO)
        ]
        fine = unfold(jnp.concatenate(rows, axis=0))
        halos.append(jnp.where(inside, coarse_ref[8 * n : 8 * n + 8, :] + fine, 0.0))
    smooth(tv_strength, where_ref, *halos, edges_ref[...], w_ref, tv_num_ref, tv_den_ref)


def sum_kernel(parts_ref, out_ref):
    block = parts_ref[0]
    for i in range(1, parts_ref.shape[0]):
        block = block + parts_ref[i]
    out_ref[...] = block


def loadings_kernel(where_ref, parts_ref, w_ref, tv_num_ref, tv_den_ref, mine_ref, got_ref, out_ref, h_ref):
    comps = w_ref.shape[1]
    half_bins = mine_ref.shape[1]
    at_first = where_ref[2] == 0
    mine, got = mine_ref[...], got_ref[...]
    h_ref[:, :half_bins] = jnp.where(at_first, mine, got)
    h_ref[:, half_bins:] = jnp.where(at_first, got, mine)
    block = parts_ref[0]
    for i in range(1, parts_ref.shape[0]):
        block = block + parts_ref[i]
    w = w_ref[...]
    fitted = jnp.dot(w, block, preferred_element_type=F32, precision=lax.Precision.HIGHEST)
    fitted = pltpu.roll(fitted, comps, 1)[:, :comps]
    out_ref[...] = w * (block[:, :comps] + tv_num_ref[...]) / (fitted + tv_den_ref[...])


def call(kernel, name, outs, in_specs, scratch=()):
    return pl.pallas_call(
        kernel,
        out_shape=tuple(jax.ShapeDtypeStruct(shape, dtype) for shape, dtype in outs),
        in_specs=in_specs,
        out_specs=(vmem(),) * len(outs),
        scratch_shapes=scratch,
        compiler_params=params(),
        name=name,
    )


def local(spectra, block_ids, counts, loadings, components):
    tile_x, tile_y, slot_count, lane = spectra.shape
    tile = tile_x * tile_y
    comps = loadings.shape[2]
    slab_bins = components.shape[1]
    half_blocks = slab_bins // lane // 2
    half_bins = half_blocks * lane
    width = ACROSS * lane
    spots = [lax.axis_index(axis) for axis in (("y", "core"), "gy", "core", "y")]
    here = jnp.stack(spots).astype(jnp.int32)
    peers = ("y", "gy")
    chunks = lax.axis_size(peers)
    pixels = spectra.transpose(0, 2, 1, 3)
    w = loadings.reshape(tile, comps)
    swap = [(0, 1), (1, 0)]
    tv_strength = tv_share * slab_bins * lax.axis_size(("w", "x"))

    keep, send = call(
        scatter_kernel,
        "scatter",
        [((half_blocks, tile, lane), BF16), ((half_blocks + 1, tile, lane), BF16)],
        [smem(), anywhere(), anywhere(), vmem(), vmem()],
        [pltpu.SMEM((slot_count,), jnp.int32), pltpu.SMEM((1,), jnp.int32), pltpu.SemaphoreType.DMA((2,))],
    )(here, block_ids.reshape(slot_count), counts.reshape(1), pixels, w)
    got = lax.ppermute(send, "core", swap)
    codes, edges = call(
        numer_kernel,
        "numer",
        [((chunks, DEPTH, width), jnp.int16), ((16, comps), F32)],
        [smem(), vmem(), vmem(), vmem()],
        [pltpu.VMEM((ACROSS, chunks * DEPTH, lane), F32)],
    )(here, keep, got, w)
    codes = lax.all_to_all(codes, peers, 0, 0, tiled=True)
    h_all, h_mine, h_send, coarse = call(
        spectra_kernel,
        "spectra",
        [((chunks, DEPTH, width), BF16), ((1, half_bins), F32), ((1, half_bins), F32), ((24, comps), F32)],
        [smem(), vmem(), vmem(), vmem(), vmem()],
        [pltpu.VMEM((1, half_bins), F32)] * 2,
    )(here, codes, edges, components, w)
    h_got = lax.ppermute(h_send, "core", swap)
    h_all = lax.all_to_all(h_all, peers, 0, 0, tiled=True)
    copies = lax.axis_size(("core", "x"))
    both, tv_num, tv_den = call(
        functools.partial(project_kernel, tv_strength),
        "project",
        [((copies, tile, 2 * comps), F32), ((tile, comps), F32), ((tile, comps), F32)],
        [smem()] + [vmem()] * 6,
        [pltpu.VMEM((ACROSS, chunks * DEPTH, lane), F32)],
    )(here, h_all, keep, got, coarse, edges, w)
    both = lax.all_to_all(both, ("core", "x"), 0, 0, tiled=True)
    (both,) = call(sum_kernel, "sum", [((tile, 2 * comps), F32)], [vmem()])(both)
    both = lax.all_gather(both, "w", axis=0)
    w_next, h_next = call(
        loadings_kernel,
        "loadings",
        [((tile, comps), F32), ((1, slab_bins), F32)],
        [smem()] + [vmem()] * 6,
    )(here, both, w, tv_num, tv_den, h_mine, h_got)
    return (w_next.reshape(tile_x, tile_y, comps), h_next)


def solution(mesh):
    gx, gy, mz = mesh.devices.shape
    fine = Mesh(mesh.devices.reshape(gx // 2, 2, gy, 4, mz // 4), ("y", "core", "gy", "w", "x"))
    rows, slabs = ("y", "core"), ("w", "x")
    in_specs = (
        P(rows, "gy", slabs, None),
        P(rows, "gy", slabs),
        P(rows, "gy", slabs),
        P(rows, "gy", None),
        P(None, slabs),
    )
    out_specs = (P(rows, "gy", None), P(("y", "core", "gy"), slabs))
    return jax.shard_map(local, mesh=fine, in_specs=in_specs, out_specs=out_specs, check_vma=False)
```

```python
import functools
import jax
import jax.numpy as jnp
from jax import lax
from jax.experimental import pallas as pl
from jax.experimental.pallas import tpu as pltpu
from jax.sharding import Mesh, PartitionSpec as P

tv_edge = 0.1
tv_share = 0.1
LANE = 128
VMEM_LIMIT = 48 * 1024 * 1024
F32 = jnp.float32
BF16 = jnp.bfloat16


def params():
    return pltpu.CompilerParams(vmem_limit_bytes=VMEM_LIMIT)


def vmem():
    return pl.BlockSpec(memory_space=pltpu.VMEM)


def smem():
    return pl.BlockSpec(memory_space=pltpu.SMEM)


def iota(shape, dim):
    return lax.broadcasted_iota(jnp.int32, shape, dim)


def nt(a, b):
    return lax.dot_general(a, b, (((1,), (1,)), ((), ())), preferred_element_type=F32)


LOG_LOW = 3.25
LOG_STEPS = 5950.0
GRAM_SCALE = 64.0
OFFSET = 32768


def encode(value):
    steps = jnp.log2(jnp.maximum(value, 1.0)) * LOG_STEPS + (1.5 - LOG_LOW * LOG_STEPS)
    return jnp.maximum(steps, 0.0).astype(jnp.int32)


def decode(code):
    steps = code.astype(jnp.int32).astype(F32) + float(OFFSET)
    return jnp.where(steps > 0.0, jnp.exp2(steps * (1.0 / LOG_STEPS) + (LOG_LOW - 1.0 / LOG_STEPS)), 0.0)


ACROSS = 13
DEPTH = 8
HALO = 4


def place_of(q):
    return divmod(q, ACROSS)


def component_of(row):
    return 8 * (row % 32 // 4) + 4 * (row // 32) + row % 4


def anywhere():
    return pl.BlockSpec(memory_space=pl.ANY)


def fetch(pairs, sems):
    copies = [pltpu.make_async_copy(source, target, sems.at[i]) for i, (source, target) in enumerate(pairs)]
    for copy in copies:
        copy.start()
    return copies


def scatter_kernel(where_ref, count_ref, ids_hbm, w_hbm, x_hbm, keep_ref, send_ref, w_ref, ids_ref, x_ref, sems):
    copies = fetch([(x_hbm, x_ref), (ids_hbm, ids_ref), (w_hbm, w_ref)], sems)
    tile_x, _, tile_y, lane = x_ref.shape
    tile = tile_x * tile_y
    half_blocks = keep_ref.shape[0]
    core = where_ref[2]
    keep_ref[...] = jnp.zeros_like(keep_ref)
    send_ref[...] = jnp.zeros_like(send_ref)
    for copy in copies:
        copy.wait()
    w = w_ref[...]
    edges = jnp.concatenate([w[:8], w[tile - 8 :]], axis=0)
    high = edges.astype(BF16).astype(F32)
    mid = (edges - high).astype(BF16).astype(F32)
    pieces = jnp.concatenate([high, mid, edges - high - mid, jnp.zeros_like(edges)], axis=0)
    send_ref[half_blocks] = jnp.concatenate([w, pieces], axis=1).astype(BF16)

    def place(s, carry):
        block = ids_ref[s]
        half = block // half_blocks
        at = block - half * half_blocks
        rows_of_slot = x_ref[:, s].astype(F32).reshape(tile, lane).astype(BF16)

        @pl.when(half == core)
        def _():
            keep_ref[at] = rows_of_slot

        @pl.when(half != core)
        def _():
            send_ref[at] = rows_of_slot

        return carry

    lax.fori_loop(0, count_ref[0], place, 0)


def put(wide_ref, q, value):
    r, j = place_of(q)
    wide_ref[j, pl.ds(r, value.shape[0], stride=DEPTH), :] = value


def numerators(w_low, dense_ref, half_blocks, wide_ref):
    comps = w_low.shape[1]
    chunks = wide_ref.shape[1] // DEPTH
    lane = LANE
    pick = jnp.where(iota((comps, comps), 1) == component_of(iota((comps, comps), 0)), 1.0, 0.0).astype(BF16)
    left = nt(pick, w_low).astype(BF16)
    for b in range(0, half_blocks, 2):
        group = range(b, min(b + 2, half_blocks))
        right = jnp.concatenate([dense_ref[i] for i in group], axis=1)
        product = jnp.dot(left, right, preferred_element_type=F32)
        for i in group:
            for m in range(2):
                part = product[m * chunks : (m + 1) * chunks, (i - b) * lane : (i - b + 1) * lane]
                put(wide_ref, m * half_blocks + i, part)
    gram = jnp.dot(left, w_low, preferred_element_type=F32) * GRAM_SCALE
    put(wide_ref, 2 * half_blocks, jnp.concatenate([gram[:chunks], gram[chunks:]], axis=1))
    for q in range(2 * half_blocks + 1, ACROSS * DEPTH):
        put(wide_ref, q, jnp.zeros((chunks, lane), F32))


def own_kernel(keep_ref, w_ref, own_ref):
    numerators(w_ref[...].astype(BF16), keep_ref, keep_ref.shape[0], own_ref)


def rims(where_ref, w, edges):
    at_first = where_ref[2] == 0
    tile = w.shape[0]
    bottom = jnp.where(at_first, edges[8:], w[tile - 8 :])
    top = jnp.where(at_first, w[:8], edges[:8])
    first = jnp.concatenate([w[8 * i : 8 * i + 1] for i in range(8)], axis=0)
    last = jnp.concatenate([w[8 * i + 7 : 8 * i + 8] for i in range(8)], axis=0)
    return [jnp.concatenate([rim[:4], rim[4:]], axis=1) for rim in (bottom, top, last, first)]


def coarse_part(value):
    return (value * 32768.0 + 0.5).astype(jnp.int32)


def rim_for(i, where_ref, values):
    side, y = where_ref[1], where_ref[3]
    to_y, to_side = divmod(i, 4)
    same_side, same_y = side == to_side, y == to_y
    out = jnp.where(jnp.logical_and(same_side, y + 1 == to_y), values[0], jnp.zeros_like(values[0]))
    out = jnp.where(jnp.logical_and(same_side, y - 1 == to_y), values[1], out)
    out = jnp.where(jnp.logical_and(same_y, side + 1 == to_side), values[2], out)
    return jnp.where(jnp.logical_and(same_y, side - 1 == to_side), values[3], out)


def rim_sources(where_ref, chunks):
    side, core, y = where_ref[1], where_ref[2], where_ref[3]
    out = []
    for from_y, from_side in ((jnp.where(core == 0, y - 1, y + 1), side), (y, side - 1), (y, side + 1)):
        inside = jnp.logical_and(
            jnp.logical_and(from_y >= 0, from_y < chunks // 4), jnp.logical_and(from_side >= 0, from_side < 4)
        )
        out.append((jnp.where(inside, from_y * 4 + from_side, 0), inside))
    return out


def unfold(rows):
    half = rows.shape[1] // 2
    return jnp.concatenate([rows[:, :half], rows[:, half:]], axis=0)


def numer_kernel(where_ref, own_ref, got_ref, w_ref, codes_ref, edges_ref, wide_ref):
    half_blocks = got_ref.shape[0] - 1
    lane = LANE
    comps = w_ref.shape[1]
    chunks = codes_ref.shape[0]
    apart = got_ref[half_blocks]
    pieces = apart[:, comps:].astype(F32)
    edges = pieces[:16] + pieces[16:32] + pieces[32:48]
    edges_ref[...] = edges
    numerators(apart[:, :comps], got_ref, half_blocks, wide_ref)

    rim_values = [coarse_part(rim) for rim in rims(where_ref, w_ref[...], edges)]
    row = iota((DEPTH, lane), 0)
    halo_row, halo_at = place_of(2 * half_blocks + 1)
    for i in range(chunks):
        rim = rim_for(i, where_ref, rim_values)
        at = slice(i * DEPTH, (i + 1) * DEPTH)
        for j in range(ACROSS):
            code = encode(own_ref[j, at, :] + wide_ref[j, at, :])
            if halo_at <= j < halo_at + HALO:
                code = jnp.where(row == halo_row, rim[j - halo_at : j - halo_at + 1], code)
            codes_ref[i, :, j * lane : (j + 1) * lane] = (code - OFFSET).astype(jnp.int16)


def spectra_kernel(
    where_ref, codes_ref, edges_ref, comps_ref, w_ref, h_all_ref, mine_ref, send_ref, coarse_ref, first_ref, second_ref
):
    lane = LANE
    chunks = codes_ref.shape[0]
    tile, comps = w_ref.shape
    half_blocks = mine_ref.shape[1] // lane
    side, core, y = where_ref[1], where_ref[2], where_ref[3]
    turn = lax.rem(8 - side, 8)
    parts = (first_ref, second_ref)

    def total(j):
        block = slice(j * lane, (j + 1) * lane)
        out = decode(codes_ref[0, :, block])
        for i in range(1, chunks):
            out = out + decode(codes_ref[i, :, block])
        return out

    sums = [total(j) for j in range(ACROSS)]
    gram_row, gram_at = place_of(2 * half_blocks)
    gram = jnp.transpose(sums[gram_at])[:, gram_row : gram_row + 1] * (1.0 / GRAM_SCALE)
    grams = [jnp.broadcast_to(gram[m * comps : (m + 1) * comps], (comps, lane)) for m in range(2)]
    halo_row, halo_at = place_of(2 * half_blocks + 1)
    w = w_ref[...]
    rim_values = [rim - coarse_part(rim).astype(F32) * (1.0 / 32768.0) for rim in rims(where_ref, w, edges_ref[...])]
    rim_low = [rim_for(i, where_ref, rim_values) for i in range(chunks)]
    row = iota((DEPTH, lane), 0)
    for j in range(ACROSS):
        denominators, own_rows = [], []
        for r in range(DEPTH):
            q = r * ACROSS + j
            if q < 2 * half_blocks:
                m, b = divmod(q, half_blocks)
                at = pl.ds(pl.multiple_of((core * half_blocks + b) * lane, lane), lane)
                denominators.append(jnp.sum(comps_ref[:, at] * grams[m], axis=0, keepdims=True))
                group = comps_ref[pl.ds(pl.multiple_of(8 * y, 8), 8), at]
                own_rows.append(pltpu.roll(group, turn, 0)[4 * m : 4 * m + 1])
            else:
                denominators.append(jnp.ones((1, lane), F32))
                own_rows.append(jnp.zeros((1, lane), F32))
        h = jnp.concatenate(own_rows, axis=0) * sums[j] / jnp.concatenate(denominators, axis=0)
        for r in range(DEPTH):
            q = r * ACROSS + j
            if q < 2 * half_blocks:
                m, b = divmod(q, half_blocks)
                parts[m][:, b * lane : (b + 1) * lane] = h[r : r + 1]
        h_low = h.astype(BF16)
        for i in range(chunks):
            if halo_at <= j < halo_at + HALO:
                rim = rim_low[i][j - halo_at : j - halo_at + 1]
                h_low = jnp.where(row == halo_row, rim, h).astype(BF16)
            h_all_ref[i, :, j * lane : (j + 1) * lane] = h_low
    mine_ref[...] = jnp.where(core == 0, first_ref[...], second_ref[...])
    send_ref[...] = jnp.where(core == 0, second_ref[...], first_ref[...])

    for n, (source, inside) in enumerate(rim_sources(where_ref, chunks)):
        rows = [
            codes_ref[source, :, j * lane : (j + 1) * lane].astype(jnp.int32)[halo_row : halo_row + 1]
            for j in range(halo_at, halo_at + HALO)
        ]
        value = (jnp.concatenate(rows, axis=0) + OFFSET).astype(F32) * (1.0 / 32768.0)
        coarse_ref[8 * n : 8 * n + 8, :] = jnp.where(inside, unfold(value), 0.0)


def smooth(tv_strength, where_ref, outer, before, after, edges, w_ref, tv_num_ref, tv_den_ref):
    comps = w_ref.shape[1]
    at_first = where_ref[2] == 0
    above = jnp.where(at_first, outer, edges[8:])
    below = jnp.where(at_first, edges[:8], outer)
    spot = iota((8, comps), 0)
    rows = [w_ref[8 * i : 8 * i + 8, :] for i in range(8)]
    for i in range(8):
        centre = rows[i]
        beside = (
            rows[i + 1] if i < 7 else below,
            rows[i - 1] if i > 0 else above,
            jnp.where(spot == 7, after[i : i + 1], pltpu.roll(centre, 7, 0)),
            jnp.where(spot == 0, before[i : i + 1], pltpu.roll(centre, 1, 0)),
        )
        num = jnp.zeros_like(centre)
        den = jnp.zeros_like(centre)
        for q in beside:
            edge_weight = 1.0 / (jnp.abs(centre - q) + tv_edge)
            num = num + edge_weight * q
            den = den + edge_weight * centre
        tv_num_ref[8 * i : 8 * i + 8, :] = tv_strength * num
        tv_den_ref[8 * i : 8 * i + 8, :] = tv_strength * den


def project_kernel(where_ref, h_ref, keep_ref, got_ref, out_ref, wide_ref):
    half_blocks, tile, lane = keep_ref.shape
    chunks = h_ref.shape[0]
    comps = 2 * chunks
    copies = out_ref.shape[0]
    core = where_ref[2]
    for j in range(ACROSS):
        block = h_ref[:, :, j * lane : (j + 1) * lane]
        wide_ref[j] = block.astype(F32).reshape(chunks * DEPTH, lane)

    def spectrum(b):
        parts = []
        for m in range(2):
            r, j = place_of(m * half_blocks + b)
            parts.append(wide_ref[j, pl.ds(r, chunks, stride=DEPTH), :])
        return jnp.concatenate(parts, axis=0).astype(BF16)

    total = jnp.zeros((2 * tile + comps, comps), F32)
    for b in range(0, half_blocks, 2):
        group = range(b, min(b + 2, half_blocks))
        h = jnp.concatenate([spectrum(i) for i in group], axis=1)
        own = jnp.concatenate([keep_ref[i] for i in group], axis=1)
        partner = jnp.concatenate([got_ref[i] for i in group], axis=1)
        total = total + nt(jnp.concatenate([own, partner, h], axis=0), h)
    name = component_of(iota((comps, lane), 0))
    to_low = jnp.where(iota((comps, lane), 1) == name, 1.0, 0.0)
    to_high = jnp.where(iota((comps, lane), 1) == name + comps, 1.0, 0.0)
    exact = dict(preferred_element_type=F32, precision=lax.Precision.HIGHEST)
    spec = lax.dot_general(to_low, total[2 * tile :], (((0,), (0,)), ((), ())), **exact)[:comps]
    spec = jnp.dot(spec, to_high, **exact)
    cross = jnp.dot(total[: 2 * tile], to_low, **exact)
    for to_core in range(2):
        both = spec + jnp.where(core == to_core, cross[:tile], cross[tile:])
        for i in range(copies // 2):
            out_ref[to_core * (copies // 2) + i] = both


def smooth_kernel(tv_strength, half_blocks, where_ref, h_ref, coarse_ref, edges_ref, w_ref, tv_num_ref, tv_den_ref):
    lane = LANE
    chunks = h_ref.shape[0]
    halo_row, halo_at = place_of(2 * half_blocks + 1)
    halos = []
    for n, (source, inside) in enumerate(rim_sources(where_ref, chunks)):
        rows = [
            h_ref[source, :, j * lane : (j + 1) * lane].astype(F32)[halo_row : halo_row + 1]
            for j in range(halo_at, halo_at + HALO)
        ]
        fine = unfold(jnp.concatenate(rows, axis=0))
        halos.append(jnp.where(inside, coarse_ref[8 * n : 8 * n + 8, :] + fine, 0.0))
    smooth(tv_strength, where_ref, *halos, edges_ref[...], w_ref, tv_num_ref, tv_den_ref)


def sum_kernel(parts_ref, out_ref):
    block = parts_ref[0]
    for i in range(1, parts_ref.shape[0]):
        block = block + parts_ref[i]
    out_ref[...] = block


def loadings_kernel(parts_ref, w_ref, tv_num_ref, tv_den_ref, out_ref):
    comps = w_ref.shape[1]
    block = parts_ref[0]
    for i in range(1, parts_ref.shape[0]):
        block = block + parts_ref[i]
    w = w_ref[...]
    fitted = jnp.dot(w, block, preferred_element_type=F32, precision=lax.Precision.HIGHEST)
    fitted = pltpu.roll(fitted, comps, 1)[:, :comps]
    out_ref[...] = w * (block[:, :comps] + tv_num_ref[...]) / (fitted + tv_den_ref[...])


def call(kernel, name, outs, in_specs, scratch=(), out_specs=None, cost=None):
    return pl.pallas_call(
        kernel,
        out_shape=tuple(jax.ShapeDtypeStruct(shape, dtype) for shape, dtype in outs),
        in_specs=in_specs,
        out_specs=out_specs or (vmem(),) * len(outs),
        scratch_shapes=scratch,
        cost_estimate=cost,
        compiler_params=params(),
        name=name,
    )


def local(spectra, block_ids, counts, loadings, components):
    tile_x, tile_y, slot_count, lane = spectra.shape
    tile = tile_x * tile_y
    comps = loadings.shape[2]
    slab_bins = components.shape[1]
    half_blocks = slab_bins // lane // 2
    half_bins = half_blocks * lane
    width = ACROSS * lane
    spots = [lax.axis_index(axis) for axis in (("y", "core"), "gy", "core", "y")]
    here = jnp.stack(spots).astype(jnp.int32)
    peers = ("y", "gy")
    chunks = lax.axis_size(peers)
    w = loadings.reshape(tile, comps)
    swap = [(0, 1), (1, 0)]
    tv_strength = tv_share * slab_bins * lax.axis_size(("w", "x"))

    in_hbm = [
        pltpu.with_memory_space_constraint(array, pltpu.HBM)
        for array in (block_ids.reshape(slot_count), w, spectra.transpose(0, 2, 1, 3))
    ]
    wide = ((ACROSS, chunks * DEPTH, lane), F32)
    keep, send, w = call(
        scatter_kernel,
        "scatter",
        [((half_blocks, tile, lane), BF16), ((half_blocks + 1, tile, lane), BF16), ((tile, comps), F32)],
        [smem(), smem(), anywhere(), anywhere(), anywhere()],
        [
            pltpu.SMEM((slot_count,), jnp.int32),
            pltpu.VMEM((tile_x, slot_count, tile_y, lane), BF16),
            pltpu.SemaphoreType.DMA((3,)),
        ],
    )(here, counts.reshape(1), *in_hbm)
    got = lax.ppermute(send, "core", swap)
    (own,) = call(
        own_kernel,
        "own",
        [wide],
        [vmem(), vmem()],
        cost=pl.CostEstimate(flops=2 * tile * comps * half_bins, bytes_accessed=4 * comps * half_bins, transcendentals=0),
    )(keep, w)
    codes, edges = call(
        numer_kernel,
        "numer",
        [((chunks, DEPTH, width), jnp.int16), ((16, comps), F32)],
        [smem(), vmem(), vmem(), vmem()],
        [pltpu.VMEM(*wide)],
    )(here, own, got, w)
    codes = lax.all_to_all(codes, peers, 0, 0, tiled=True)
    h_all, h_mine, h_send, coarse = call(
        spectra_kernel,
        "spectra",
        [((chunks, DEPTH, width), BF16), ((1, half_bins), F32), ((1, half_bins), F32), ((24, comps), F32)],
        [smem(), vmem(), vmem(), vmem(), vmem()],
        [pltpu.VMEM((1, half_bins), F32)] * 2,
    )(here, codes, edges, components, w)
    h_got = lax.ppermute(h_send, "core", swap)
    h_all = lax.all_to_all(h_all, peers, 0, 0, tiled=True)
    copies = lax.axis_size(("core", "x"))
    (both,) = call(
        project_kernel,
        "project",
        [((copies, tile, 2 * comps), F32)],
        [smem(), vmem(), vmem(), vmem()],
        [pltpu.VMEM(*wide)],
    )(here, h_all, keep, got)
    tv_num, tv_den = call(
        functools.partial(smooth_kernel, tv_strength, half_blocks),
        "smooth",
        [((tile, comps), F32)] * 2,
        [smem()] + [vmem()] * 4,
        cost=pl.CostEstimate(flops=80 * tile * comps, bytes_accessed=64 * tile * comps, transcendentals=8 * tile * comps),
    )(here, h_all, coarse, edges, w)
    both = lax.all_to_all(both, ("core", "x"), 0, 0, tiled=True)
    (both,) = call(sum_kernel, "sum", [((tile, 2 * comps), F32)], [vmem()])(both)
    both = lax.all_gather(both, "w", axis=0)
    (w_next,) = call(loadings_kernel, "loadings", [((tile, comps), F32)], [vmem()] * 4)(both, w, tv_num, tv_den)
    h_pair = jnp.concatenate([h_got, h_mine, h_got], axis=1)
    h_next = lax.dynamic_slice_in_dim(h_pair, (1 - lax.axis_index("core")) * half_bins, slab_bins, 1)
    return (w_next.reshape(tile_x, tile_y, comps), h_next)


def solution(mesh):
    gx, gy, mz = mesh.devices.shape
    fine = Mesh(mesh.devices.reshape(gx // 2, 2, gy, 4, mz // 4), ("y", "core", "gy", "w", "x"))
    rows, slabs = ("y", "core"), ("w", "x")
    in_specs = (
        P(rows, "gy", slabs, None),
        P(rows, "gy", slabs),
        P(rows, "gy", slabs),
        P(rows, "gy", None),
        P(None, slabs),
    )
    out_specs = (P(rows, "gy", None), P(("y", "core", "gy"), slabs))
    return jax.shard_map(local, mesh=fine, in_specs=in_specs, out_specs=out_specs, check_vma=False)
```

```python
import functools
import jax
import jax.numpy as jnp
from jax import lax
from jax.experimental import pallas as pl
from jax.experimental.pallas import tpu as pltpu
from jax.sharding import Mesh, PartitionSpec as P

tv_edge = 0.1
tv_share = 0.1
LANE = 128
VMEM_LIMIT = 48 * 1024 * 1024
F32 = jnp.float32
BF16 = jnp.bfloat16


def params():
    return pltpu.CompilerParams(vmem_limit_bytes=VMEM_LIMIT)


def vmem():
    return pl.BlockSpec(memory_space=pltpu.VMEM)


def smem():
    return pl.BlockSpec(memory_space=pltpu.SMEM)


def iota(shape, dim):
    return lax.broadcasted_iota(jnp.int32, shape, dim)


def nt(a, b):
    return lax.dot_general(a, b, (((1,), (1,)), ((), ())), preferred_element_type=F32)


LOG_LOW = 3.25
LOG_STEPS = 5950.0
GRAM_SCALE = 64.0
OFFSET = 32768


def encode(value):
    steps = jnp.log2(jnp.maximum(value, 1.0)) * LOG_STEPS + (1.5 - LOG_LOW * LOG_STEPS)
    return jnp.maximum(steps, 0.0).astype(jnp.int32)


def decode(code):
    steps = code.astype(jnp.int32).astype(F32) + float(OFFSET)
    return jnp.where(steps > 0.0, jnp.exp2(steps * (1.0 / LOG_STEPS) + (LOG_LOW - 1.0 / LOG_STEPS)), 0.0)


ACROSS = 13
DEPTH = 8
HALO = 4


def place_of(q):
    return divmod(q, ACROSS)


def component_of(row):
    return 8 * (row % 32 // 4) + 4 * (row // 32) + row % 4


def anywhere():
    return pl.BlockSpec(memory_space=pl.ANY)


def fetch(pairs, sems):
    copies = [pltpu.make_async_copy(source, target, sems.at[i]) for i, (source, target) in enumerate(pairs)]
    for copy in copies:
        copy.start()
    return copies


def scatter_kernel(where_ref, count_ref, ids_hbm, w_hbm, x_hbm, keep_ref, send_ref, w_ref, ids_ref, x_ref, sems):
    copies = fetch([(x_hbm, x_ref), (ids_hbm, ids_ref), (w_hbm, w_ref)], sems)
    tile_x, _, tile_y, lane = x_ref.shape
    tile = tile_x * tile_y
    half_blocks = keep_ref.shape[0]
    core = where_ref[2]
    keep_ref[...] = jnp.zeros_like(keep_ref)
    send_ref[...] = jnp.zeros_like(send_ref)
    for copy in copies:
        copy.wait()
    w = w_ref[...]
    edges = jnp.concatenate([w[:8], w[tile - 8 :]], axis=0)
    high = edges.astype(BF16).astype(F32)
    mid = (edges - high).astype(BF16).astype(F32)
    pieces = jnp.concatenate([high, mid, edges - high - mid, jnp.zeros_like(edges)], axis=0)
    send_ref[half_blocks] = jnp.concatenate([w, pieces], axis=1).astype(BF16)

    def place(s, carry):
        block = ids_ref[s]
        half = block // half_blocks
        at = block - half * half_blocks
        rows_of_slot = x_ref[:, s].astype(F32).reshape(tile, lane).astype(BF16)

        @pl.when(half == core)
        def _():
            keep_ref[at] = rows_of_slot

        @pl.when(half != core)
        def _():
            send_ref[at] = rows_of_slot

        return carry

    lax.fori_loop(0, count_ref[0], place, 0)


def put(wide_ref, q, value):
    r, j = place_of(q)
    wide_ref[j, pl.ds(r, value.shape[0], stride=DEPTH), :] = value


def numerators(w_low, dense_ref, half_blocks, wide_ref):
    comps = w_low.shape[1]
    chunks = wide_ref.shape[1] // DEPTH
    lane = LANE
    pick = jnp.where(iota((comps, comps), 1) == component_of(iota((comps, comps), 0)), 1.0, 0.0).astype(BF16)
    left = nt(pick, w_low).astype(BF16)
    for b in range(0, half_blocks, 2):
        group = range(b, min(b + 2, half_blocks))
        right = jnp.concatenate([dense_ref[i] for i in group], axis=1)
        product = jnp.dot(left, right, preferred_element_type=F32)
        for i in group:
            for m in range(2):
                part = product[m * chunks : (m + 1) * chunks, (i - b) * lane : (i - b + 1) * lane]
                put(wide_ref, m * half_blocks + i, part)
    gram = jnp.dot(left, w_low, preferred_element_type=F32) * GRAM_SCALE
    put(wide_ref, 2 * half_blocks, jnp.concatenate([gram[:chunks], gram[chunks:]], axis=1))
    for q in range(2 * half_blocks + 1, ACROSS * DEPTH):
        put(wide_ref, q, jnp.zeros((chunks, lane), F32))


def own_kernel(keep_ref, w_ref, own_ref):
    numerators(w_ref[...].astype(BF16), keep_ref, keep_ref.shape[0], own_ref)


def rims(where_ref, w, edges):
    at_first = where_ref[2] == 0
    tile = w.shape[0]
    bottom = jnp.where(at_first, edges[8:], w[tile - 8 :])
    top = jnp.where(at_first, w[:8], edges[:8])
    first = jnp.concatenate([w[8 * i : 8 * i + 1] for i in range(8)], axis=0)
    last = jnp.concatenate([w[8 * i + 7 : 8 * i + 8] for i in range(8)], axis=0)
    return [jnp.concatenate([rim[:4], rim[4:]], axis=1) for rim in (bottom, top, last, first)]


def coarse_part(value):
    return (value * 32768.0 + 0.5).astype(jnp.int32)


def rim_for(i, where_ref, values):
    side, y = where_ref[1], where_ref[3]
    to_y, to_side = divmod(i, 4)
    same_side, same_y = side == to_side, y == to_y
    out = jnp.where(jnp.logical_and(same_side, y + 1 == to_y), values[0], jnp.zeros_like(values[0]))
    out = jnp.where(jnp.logical_and(same_side, y - 1 == to_y), values[1], out)
    out = jnp.where(jnp.logical_and(same_y, side + 1 == to_side), values[2], out)
    return jnp.where(jnp.logical_and(same_y, side - 1 == to_side), values[3], out)


def rim_sources(where_ref, chunks):
    side, core, y = where_ref[1], where_ref[2], where_ref[3]
    out = []
    for from_y, from_side in ((jnp.where(core == 0, y - 1, y + 1), side), (y, side - 1), (y, side + 1)):
        inside = jnp.logical_and(
            jnp.logical_and(from_y >= 0, from_y < chunks // 4), jnp.logical_and(from_side >= 0, from_side < 4)
        )
        out.append((jnp.where(inside, from_y * 4 + from_side, 0), inside))
    return out


def unfold(rows):
    half = rows.shape[1] // 2
    return jnp.concatenate([rows[:, :half], rows[:, half:]], axis=0)


def numer_kernel(where_ref, own_ref, got_ref, w_ref, codes_ref, edges_ref, wide_ref):
    half_blocks = got_ref.shape[0] - 1
    lane = LANE
    comps = w_ref.shape[1]
    chunks = codes_ref.shape[0]
    apart = got_ref[half_blocks]
    pieces = apart[:, comps:].astype(F32)
    edges = pieces[:16] + pieces[16:32] + pieces[32:48]
    edges_ref[...] = edges
    numerators(apart[:, :comps], got_ref, half_blocks, wide_ref)

    rim_values = [coarse_part(rim) for rim in rims(where_ref, w_ref[...], edges)]
    row = iota((DEPTH, lane), 0)
    halo_row, halo_at = place_of(2 * half_blocks + 1)
    for i in range(chunks):
        rim = rim_for(i, where_ref, rim_values)
        at = slice(i * DEPTH, (i + 1) * DEPTH)
        for j in range(ACROSS):
            code = encode(own_ref[j, at, :] + wide_ref[j, at, :])
            if halo_at <= j < halo_at + HALO:
                code = jnp.where(row == halo_row, rim[j - halo_at : j - halo_at + 1], code)
            codes_ref[i, :, j * lane : (j + 1) * lane] = (code - OFFSET).astype(jnp.int16)


def spectra_kernel(
    where_ref, codes_ref, edges_ref, comps_ref, w_ref, h_all_ref, mine_ref, send_ref, coarse_ref, first_ref, second_ref
):
    lane = LANE
    chunks = codes_ref.shape[0]
    tile, comps = w_ref.shape
    half_blocks = mine_ref.shape[1] // lane
    side, core, y = where_ref[1], where_ref[2], where_ref[3]
    turn = lax.rem(8 - side, 8)
    parts = (first_ref, second_ref)

    def total(j):
        block = slice(j * lane, (j + 1) * lane)
        out = decode(codes_ref[0, :, block])
        for i in range(1, chunks):
            out = out + decode(codes_ref[i, :, block])
        return out

    sums = [total(j) for j in range(ACROSS)]
    gram_row, gram_at = place_of(2 * half_blocks)
    gram = jnp.transpose(sums[gram_at])[:, gram_row : gram_row + 1] * (1.0 / GRAM_SCALE)
    grams = [jnp.broadcast_to(gram[m * comps : (m + 1) * comps], (comps, lane)) for m in range(2)]
    halo_row, halo_at = place_of(2 * half_blocks + 1)
    w = w_ref[...]
    rim_values = [rim - coarse_part(rim).astype(F32) * (1.0 / 32768.0) for rim in rims(where_ref, w, edges_ref[...])]
    rim_low = [rim_for(i, where_ref, rim_values) for i in range(chunks)]
    row = iota((DEPTH, lane), 0)
    for j in range(ACROSS):
        denominators, own_rows = [], []
        for r in range(DEPTH):
            q = r * ACROSS + j
            if q < 2 * half_blocks:
                m, b = divmod(q, half_blocks)
                at = pl.ds(pl.multiple_of((core * half_blocks + b) * lane, lane), lane)
                denominators.append(jnp.sum(comps_ref[:, at] * grams[m], axis=0, keepdims=True))
                group = comps_ref[pl.ds(pl.multiple_of(8 * y, 8), 8), at]
                own_rows.append(pltpu.roll(group, turn, 0)[4 * m : 4 * m + 1])
            else:
                denominators.append(jnp.ones((1, lane), F32))
                own_rows.append(jnp.zeros((1, lane), F32))
        h = jnp.concatenate(own_rows, axis=0) * sums[j] / jnp.concatenate(denominators, axis=0)
        for r in range(DEPTH):
            q = r * ACROSS + j
            if q < 2 * half_blocks:
                m, b = divmod(q, half_blocks)
                parts[m][:, b * lane : (b + 1) * lane] = h[r : r + 1]
        h_low = h.astype(BF16)
        for i in range(chunks):
            if halo_at <= j < halo_at + HALO:
                rim = rim_low[i][j - halo_at : j - halo_at + 1]
                h_low = jnp.where(row == halo_row, rim, h).astype(BF16)
            h_all_ref[i, :, j * lane : (j + 1) * lane] = h_low
    mine_ref[...] = jnp.where(core == 0, first_ref[...], second_ref[...])
    send_ref[...] = jnp.where(core == 0, second_ref[...], first_ref[...])

    for n, (source, inside) in enumerate(rim_sources(where_ref, chunks)):
        rows = [
            codes_ref[source, :, j * lane : (j + 1) * lane].astype(jnp.int32)[halo_row : halo_row + 1]
            for j in range(halo_at, halo_at + HALO)
        ]
        value = (jnp.concatenate(rows, axis=0) + OFFSET).astype(F32) * (1.0 / 32768.0)
        coarse_ref[8 * n : 8 * n + 8, :] = jnp.where(inside, unfold(value), 0.0)


def smooth(tv_strength, where_ref, outer, before, after, edges, w_ref, tv_num_ref, tv_den_ref):
    comps = w_ref.shape[1]
    at_first = where_ref[2] == 0
    above = jnp.where(at_first, outer, edges[8:])
    below = jnp.where(at_first, edges[:8], outer)
    spot = iota((8, comps), 0)
    rows = [w_ref[8 * i : 8 * i + 8, :] for i in range(8)]
    for i in range(8):
        centre = rows[i]
        beside = (
            rows[i + 1] if i < 7 else below,
            rows[i - 1] if i > 0 else above,
            jnp.where(spot == 7, after[i : i + 1], pltpu.roll(centre, 7, 0)),
            jnp.where(spot == 0, before[i : i + 1], pltpu.roll(centre, 1, 0)),
        )
        num = jnp.zeros_like(centre)
        den = jnp.zeros_like(centre)
        for q in beside:
            edge_weight = 1.0 / (jnp.abs(centre - q) + tv_edge)
            num = num + edge_weight * q
            den = den + edge_weight * centre
        tv_num_ref[8 * i : 8 * i + 8, :] = tv_strength * num
        tv_den_ref[8 * i : 8 * i + 8, :] = tv_strength * den


def project_kernel(
    tv_strength, where_ref, h_ref, keep_ref, got_ref, coarse_ref, edges_ref, w_ref, out_ref, tv_num_ref, tv_den_ref, wide_ref
):
    half_blocks, tile, lane = keep_ref.shape
    chunks = h_ref.shape[0]
    comps = 2 * chunks
    copies = out_ref.shape[0]
    core = where_ref[2]
    for j in range(ACROSS):
        block = h_ref[:, :, j * lane : (j + 1) * lane]
        wide_ref[j] = block.astype(F32).reshape(chunks * DEPTH, lane)

    def spectrum(b):
        parts = []
        for m in range(2):
            r, j = place_of(m * half_blocks + b)
            parts.append(wide_ref[j, pl.ds(r, chunks, stride=DEPTH), :])
        return jnp.concatenate(parts, axis=0).astype(BF16)

    total = jnp.zeros((2 * tile + comps, comps), F32)
    for b in range(0, half_blocks, 2):
        group = range(b, min(b + 2, half_blocks))
        h = jnp.concatenate([spectrum(i) for i in group], axis=1)
        own = jnp.concatenate([keep_ref[i] for i in group], axis=1)
        partner = jnp.concatenate([got_ref[i] for i in group], axis=1)
        total = total + nt(jnp.concatenate([own, partner, h], axis=0), h)
    name = component_of(iota((comps, lane), 0))
    to_low = jnp.where(iota((comps, lane), 1) == name, 1.0, 0.0)
    to_high = jnp.where(iota((comps, lane), 1) == name + comps, 1.0, 0.0)
    exact = dict(preferred_element_type=F32, precision=lax.Precision.HIGHEST)
    spec = lax.dot_general(to_low, total[2 * tile :], (((0,), (0,)), ((), ())), **exact)[:comps]
    spec = jnp.dot(spec, to_high, **exact)
    cross = jnp.dot(total[: 2 * tile], to_low, **exact)
    for to_core in range(2):
        both = spec + jnp.where(core == to_core, cross[:tile], cross[tile:])
        for i in range(copies // 2):
            out_ref[to_core * (copies // 2) + i] = both

    halo_row, halo_at = place_of(2 * half_blocks + 1)
    halos = []
    for n, (source, inside) in enumerate(rim_sources(where_ref, chunks)):
        rows = [
            h_ref[source, :, j * lane : (j + 1) * lane].astype(F32)[halo_row : halo_row + 1]
            for j in range(halo_at, halo_at + HALO)
        ]
        fine = unfold(jnp.concatenate(rows, axis=0))
        halos.append(jnp.where(inside, coarse_ref[8 * n : 8 * n + 8, :] + fine, 0.0))
    smooth(tv_strength, where_ref, *halos, edges_ref[...], w_ref, tv_num_ref, tv_den_ref)


def sum_kernel(parts_ref, out_ref):
    block = parts_ref[0]
    for i in range(1, parts_ref.shape[0]):
        block = block + parts_ref[i]
    out_ref[...] = block


def loadings_kernel(parts_ref, w_ref, tv_num_ref, tv_den_ref, out_ref):
    comps = w_ref.shape[1]
    block = parts_ref[0]
    for i in range(1, parts_ref.shape[0]):
        block = block + parts_ref[i]
    w = w_ref[...]
    fitted = jnp.dot(w, block, preferred_element_type=F32, precision=lax.Precision.HIGHEST)
    fitted = pltpu.roll(fitted, comps, 1)[:, :comps]
    out_ref[...] = w * (block[:, :comps] + tv_num_ref[...]) / (fitted + tv_den_ref[...])


def call(kernel, name, outs, in_specs, scratch=(), out_specs=None, cost=None):
    return pl.pallas_call(
        kernel,
        out_shape=tuple(jax.ShapeDtypeStruct(shape, dtype) for shape, dtype in outs),
        in_specs=in_specs,
        out_specs=out_specs or (vmem(),) * len(outs),
        scratch_shapes=scratch,
        cost_estimate=cost,
        compiler_params=params(),
        name=name,
    )


def local(spectra, block_ids, counts, loadings, components):
    tile_x, tile_y, slot_count, lane = spectra.shape
    tile = tile_x * tile_y
    comps = loadings.shape[2]
    slab_bins = components.shape[1]
    half_blocks = slab_bins // lane // 2
    half_bins = half_blocks * lane
    width = ACROSS * lane
    spots = [lax.axis_index(axis) for axis in (("y", "core"), "gy", "core", "y")]
    here = jnp.stack(spots).astype(jnp.int32)
    peers = ("y", "gy")
    chunks = lax.axis_size(peers)
    w = loadings.reshape(tile, comps)
    swap = [(0, 1), (1, 0)]
    tv_strength = tv_share * slab_bins * lax.axis_size(("w", "x"))

    in_hbm = [
        pltpu.with_memory_space_constraint(array, pltpu.HBM)
        for array in (block_ids.reshape(slot_count), w, spectra.transpose(0, 2, 1, 3))
    ]
    wide = ((ACROSS, chunks * DEPTH, lane), F32)
    keep, send, w = call(
        scatter_kernel,
        "scatter",
        [((half_blocks, tile, lane), BF16), ((half_blocks + 1, tile, lane), BF16), ((tile, comps), F32)],
        [smem(), smem(), anywhere(), anywhere(), anywhere()],
        [
            pltpu.SMEM((slot_count,), jnp.int32),
            pltpu.VMEM((tile_x, slot_count, tile_y, lane), BF16),
            pltpu.SemaphoreType.DMA((3,)),
        ],
    )(here, counts.reshape(1), *in_hbm)
    got = lax.ppermute(send, "core", swap)
    (own,) = call(
        own_kernel,
        "own",
        [wide],
        [vmem(), vmem()],
        cost=pl.CostEstimate(flops=2 * tile * comps * half_bins, bytes_accessed=4 * comps * half_bins, transcendentals=0),
    )(keep, w)
    codes, edges = call(
        numer_kernel,
        "numer",
        [((chunks, DEPTH, width), jnp.int16), ((16, comps), F32)],
        [smem(), vmem(), vmem(), vmem()],
        [pltpu.VMEM(*wide)],
    )(here, own, got, w)
    codes = lax.all_to_all(codes, peers, 0, 0, tiled=True)
    h_all, h_mine, h_send, coarse = call(
        spectra_kernel,
        "spectra",
        [((chunks, DEPTH, width), BF16), ((1, half_bins), F32), ((1, half_bins), F32), ((24, comps), F32)],
        [smem(), vmem(), vmem(), vmem(), vmem()],
        [pltpu.VMEM((1, half_bins), F32)] * 2,
    )(here, codes, edges, components, w)
    h_got = lax.ppermute(h_send, "core", swap)
    h_all = lax.all_to_all(h_all, peers, 0, 0, tiled=True)
    copies = lax.axis_size(("core", "x"))
    h_pair = jnp.concatenate([h_got, h_mine, h_got], axis=1)
    h_next = lax.dynamic_slice_in_dim(h_pair, (1 - lax.axis_index("core")) * half_bins, slab_bins, 1)
    h_all, h_next = lax.optimization_barrier((h_all, h_next))
    both, tv_num, tv_den = call(
        functools.partial(project_kernel, tv_strength),
        "project",
        [((copies, tile, 2 * comps), F32), ((tile, comps), F32), ((tile, comps), F32)],
        [smem()] + [vmem()] * 6,
        [pltpu.VMEM(*wide)],
    )(here, h_all, keep, got, coarse, edges, w)
    both = lax.all_to_all(both, ("core", "x"), 0, 0, tiled=True)
    (both,) = call(sum_kernel, "sum", [((tile, 2 * comps), F32)], [vmem()])(both)
    both = lax.all_gather(both, "w", axis=0)
    (w_next,) = call(loadings_kernel, "loadings", [((tile, comps), F32)], [vmem()] * 4)(both, w, tv_num, tv_den)
    return (w_next.reshape(tile_x, tile_y, comps), h_next)


def solution(mesh):
    gx, gy, mz = mesh.devices.shape
    fine = Mesh(mesh.devices.reshape(gx // 2, 2, gy, 4, mz // 4), ("y", "core", "gy", "w", "x"))
    rows, slabs = ("y", "core"), ("w", "x")
    in_specs = (
        P(rows, "gy", slabs, None),
        P(rows, "gy", slabs),
        P(rows, "gy", slabs),
        P(rows, "gy", None),
        P(None, slabs),
    )
    out_specs = (P(rows, "gy", None), P(("y", "core", "gy"), slabs))
    return jax.shard_map(local, mesh=fine, in_specs=in_specs, out_specs=out_specs, check_vma=False)
```

```python
import functools
import math
import jax
import jax.numpy as jnp
from jax import lax
from jax.experimental import pallas as pl
from jax.experimental.pallas import tpu as pltpu
from jax.sharding import Mesh, PartitionSpec as P

tv_edge = 0.1
tv_share = 0.1
LANE = 128
VMEM_LIMIT = 48 * 1024 * 1024
F32 = jnp.float32
BF16 = jnp.bfloat16


def params():
    return pltpu.CompilerParams(vmem_limit_bytes=VMEM_LIMIT)


def vmem():
    return pl.BlockSpec(memory_space=pltpu.VMEM)


def smem():
    return pl.BlockSpec(memory_space=pltpu.SMEM)


def iota(shape, dim):
    return lax.broadcasted_iota(jnp.int32, shape, dim)


def nt(a, b):
    return lax.dot_general(a, b, (((1,), (1,)), ((), ())), preferred_element_type=F32)


LOG_LOW = 3.25
LOG_STEPS = 5950.0
GRAM_SCALE = 64.0
OFFSET = 32768


def encode(value):
    steps = jnp.log2(jnp.maximum(value, 1.0)) * LOG_STEPS + (1.5 - LOG_LOW * LOG_STEPS)
    return jnp.maximum(steps, 0.0).astype(jnp.int32)


def decode(code):
    steps = code.astype(jnp.int32).astype(F32) + float(OFFSET)
    return jnp.where(steps > 0.0, jnp.exp2(steps * (1.0 / LOG_STEPS) + (LOG_LOW - 1.0 / LOG_STEPS)), 0.0)


ACROSS = 13
SPARE = 2
DEPTH = 8
HALO = 4


def place_of(q):
    return divmod(q, ACROSS)


def component_of(row):
    return 8 * (row % 32 // 4) + 4 * (row // 32) + row % 4


def anywhere():
    return pl.BlockSpec(memory_space=pl.ANY)


def fetch(pairs, sems):
    copies = [pltpu.make_async_copy(source, target, sems.at[i]) for i, (source, target) in enumerate(pairs)]
    for copy in copies:
        copy.start()
    return copies


def scatter_kernel(where_ref, count_ref, ids_hbm, w_hbm, x_hbm, keep_ref, send_ref, w_ref, ids_ref, x_ref, sems):
    copies = fetch([(x_hbm, x_ref), (ids_hbm, ids_ref), (w_hbm, w_ref)], sems)
    tile_x, slots, tile_y, lane = x_ref.shape
    tile = tile_x * tile_y
    half_blocks = keep_ref.shape[0] - SPARE
    spill = half_blocks + 1
    core, count = where_ref[2], count_ref[0]
    keep_ref[...] = jnp.zeros_like(keep_ref)
    send_ref[...] = jnp.zeros_like(send_ref)
    for copy in copies:
        copy.wait()
    w = w_ref[...]
    edges = jnp.concatenate([w[:8], w[tile - 8 :]], axis=0)
    high = edges.astype(BF16).astype(F32)
    mid = (edges - high).astype(BF16).astype(F32)
    pieces = jnp.concatenate([high, mid, edges - high - mid, jnp.zeros_like(edges)], axis=0)
    send_ref[half_blocks] = jnp.concatenate([w, pieces], axis=1).astype(BF16)

    def place(s):
        block = ids_ref[s]
        upper = block >= half_blocks
        at = jnp.where(s < count, jnp.where(upper, block - half_blocks, block), spill)
        rows_of_slot = x_ref[:, s].astype(F32).reshape(tile, lane).astype(BF16)
        here = upper == (core == 1)
        keep_ref[jnp.where(here, at, spill)] = rows_of_slot
        send_ref[jnp.where(here, spill, at)] = rows_of_slot

    def place_group(g, carry):
        for i in range(group):
            place(g * group + i)
        return carry

    group = math.gcd(slots, 4)
    lax.fori_loop(0, (count + group - 1) // group, place_group, 0)


def put(wide_ref, q, value):
    r, j = place_of(q)
    wide_ref[j, pl.ds(r, value.shape[0], stride=DEPTH), :] = value


def numerators(w_low, dense_ref, half_blocks, wide_ref):
    comps = w_low.shape[1]
    chunks = wide_ref.shape[1] // DEPTH
    lane = LANE
    pick = jnp.where(iota((comps, comps), 1) == component_of(iota((comps, comps), 0)), 1.0, 0.0).astype(BF16)
    left = nt(pick, w_low).astype(BF16)
    for b in range(0, half_blocks, 2):
        group = range(b, min(b + 2, half_blocks))
        right = jnp.concatenate([dense_ref[i] for i in group], axis=1)
        product = jnp.dot(left, right, preferred_element_type=F32)
        for i in group:
            for m in range(2):
                part = product[m * chunks : (m + 1) * chunks, (i - b) * lane : (i - b + 1) * lane]
                put(wide_ref, m * half_blocks + i, part)
    gram = jnp.dot(left, w_low, preferred_element_type=F32) * GRAM_SCALE
    put(wide_ref, 2 * half_blocks, jnp.concatenate([gram[:chunks], gram[chunks:]], axis=1))
    for q in range(2 * half_blocks + 1, ACROSS * DEPTH):
        put(wide_ref, q, jnp.zeros((chunks, lane), F32))


def own_kernel(keep_ref, w_ref, own_ref):
    numerators(w_ref[...].astype(BF16), keep_ref, keep_ref.shape[0] - SPARE, own_ref)


def rims(where_ref, w, edges):
    at_first = where_ref[2] == 0
    tile = w.shape[0]
    bottom = jnp.where(at_first, edges[8:], w[tile - 8 :])
    top = jnp.where(at_first, w[:8], edges[:8])
    first = jnp.concatenate([w[8 * i : 8 * i + 1] for i in range(8)], axis=0)
    last = jnp.concatenate([w[8 * i + 7 : 8 * i + 8] for i in range(8)], axis=0)
    return [jnp.concatenate([rim[:4], rim[4:]], axis=1) for rim in (bottom, top, last, first)]


def coarse_part(value):
    return (value * 32768.0 + 0.5).astype(jnp.int32)


def rim_for(i, where_ref, values):
    side, y = where_ref[1], where_ref[3]
    to_y, to_side = divmod(i, 4)
    same_side, same_y = side == to_side, y == to_y
    out = jnp.where(jnp.logical_and(same_side, y + 1 == to_y), values[0], jnp.zeros_like(values[0]))
    out = jnp.where(jnp.logical_and(same_side, y - 1 == to_y), values[1], out)
    out = jnp.where(jnp.logical_and(same_y, side + 1 == to_side), values[2], out)
    return jnp.where(jnp.logical_and(same_y, side - 1 == to_side), values[3], out)


def rim_sources(where_ref, chunks):
    side, core, y = where_ref[1], where_ref[2], where_ref[3]
    out = []
    for from_y, from_side in ((jnp.where(core == 0, y - 1, y + 1), side), (y, side - 1), (y, side + 1)):
        inside = jnp.logical_and(
            jnp.logical_and(from_y >= 0, from_y < chunks // 4), jnp.logical_and(from_side >= 0, from_side < 4)
        )
        out.append((jnp.where(inside, from_y * 4 + from_side, 0), inside))
    return out


def unfold(rows):
    half = rows.shape[1] // 2
    return jnp.concatenate([rows[:, :half], rows[:, half:]], axis=0)


def numer_kernel(where_ref, own_ref, got_ref, w_ref, codes_ref, edges_ref, wide_ref):
    half_blocks = got_ref.shape[0] - SPARE
    lane = LANE
    comps = w_ref.shape[1]
    chunks = codes_ref.shape[0]
    apart = got_ref[half_blocks]
    pieces = apart[:, comps:].astype(F32)
    edges = pieces[:16] + pieces[16:32] + pieces[32:48]
    edges_ref[...] = edges
    numerators(apart[:, :comps], got_ref, half_blocks, wide_ref)

    rim_values = [coarse_part(rim) for rim in rims(where_ref, w_ref[...], edges)]
    row = iota((DEPTH, lane), 0)
    halo_row, halo_at = place_of(2 * half_blocks + 1)
    for i in range(chunks):
        rim = rim_for(i, where_ref, rim_values)
        at = slice(i * DEPTH, (i + 1) * DEPTH)
        for j in range(ACROSS):
            code = encode(own_ref[j, at, :] + wide_ref[j, at, :])
            if halo_at <= j < halo_at + HALO:
                code = jnp.where(row == halo_row, rim[j - halo_at : j - halo_at + 1], code)
            codes_ref[i, :, j * lane : (j + 1) * lane] = (code - OFFSET).astype(jnp.int16)


def spectra_kernel(
    where_ref, codes_ref, edges_ref, comps_ref, w_ref, h_all_ref, mine_ref, send_ref, coarse_ref, first_ref, second_ref
):
    lane = LANE
    chunks = codes_ref.shape[0]
    tile, comps = w_ref.shape
    half_blocks = mine_ref.shape[1] // lane
    side, core, y = where_ref[1], where_ref[2], where_ref[3]
    turn = lax.rem(8 - side, 8)
    parts = (first_ref, second_ref)

    def total(j):
        block = slice(j * lane, (j + 1) * lane)
        out = decode(codes_ref[0, :, block])
        for i in range(1, chunks):
            out = out + decode(codes_ref[i, :, block])
        return out

    sums = [total(j) for j in range(ACROSS)]
    gram_row, gram_at = place_of(2 * half_blocks)
    gram = jnp.transpose(sums[gram_at])[:, gram_row : gram_row + 1] * (1.0 / GRAM_SCALE)
    grams = [jnp.broadcast_to(gram[m * comps : (m + 1) * comps], (comps, lane)) for m in range(2)]
    halo_row, halo_at = place_of(2 * half_blocks + 1)
    w = w_ref[...]
    rim_values = [rim - coarse_part(rim).astype(F32) * (1.0 / 32768.0) for rim in rims(where_ref, w, edges_ref[...])]
    rim_low = [rim_for(i, where_ref, rim_values) for i in range(chunks)]
    row = iota((DEPTH, lane), 0)
    for j in range(ACROSS):
        denominators, own_rows = [], []
        for r in range(DEPTH):
            q = r * ACROSS + j
            if q < 2 * half_blocks:
                m, b = divmod(q, half_blocks)
                at = pl.ds(pl.multiple_of((core * half_blocks + b) * lane, lane), lane)
                denominators.append(jnp.sum(comps_ref[:, at] * grams[m], axis=0, keepdims=True))
                group = comps_ref[pl.ds(pl.multiple_of(8 * y, 8), 8), at]
                own_rows.append(pltpu.roll(group, turn, 0)[4 * m : 4 * m + 1])
            else:
                denominators.append(jnp.ones((1, lane), F32))
                own_rows.append(jnp.zeros((1, lane), F32))
        h = jnp.concatenate(own_rows, axis=0) * sums[j] / jnp.concatenate(denominators, axis=0)
        for r in range(DEPTH):
            q = r * ACROSS + j
            if q < 2 * half_blocks:
                m, b = divmod(q, half_blocks)
                parts[m][:, b * lane : (b + 1) * lane] = h[r : r + 1]
        h_low = h.astype(BF16)
        for i in range(chunks):
            if halo_at <= j < halo_at + HALO:
                rim = rim_low[i][j - halo_at : j - halo_at + 1]
                h_low = jnp.where(row == halo_row, rim, h).astype(BF16)
            h_all_ref[i, :, j * lane : (j + 1) * lane] = h_low
    mine_ref[...] = jnp.where(core == 0, first_ref[...], second_ref[...])
    send_ref[...] = jnp.where(core == 0, second_ref[...], first_ref[...])

    for n, (source, inside) in enumerate(rim_sources(where_ref, chunks)):
        rows = [
            codes_ref[source, :, j * lane : (j + 1) * lane].astype(jnp.int32)[halo_row : halo_row + 1]
            for j in range(halo_at, halo_at + HALO)
        ]
        value = (jnp.concatenate(rows, axis=0) + OFFSET).astype(F32) * (1.0 / 32768.0)
        coarse_ref[8 * n : 8 * n + 8, :] = jnp.where(inside, unfold(value), 0.0)


def smooth(tv_strength, where_ref, outer, before, after, edges, w_ref, tv_num_ref, tv_den_ref):
    comps = w_ref.shape[1]
    at_first = where_ref[2] == 0
    above = jnp.where(at_first, outer, edges[8:])
    below = jnp.where(at_first, edges[:8], outer)
    spot = iota((8, comps), 0)
    rows = [w_ref[8 * i : 8 * i + 8, :] for i in range(8)]
    for i in range(8):
        centre = rows[i]
        beside = (
            rows[i + 1] if i < 7 else below,
            rows[i - 1] if i > 0 else above,
            jnp.where(spot == 7, after[i : i + 1], pltpu.roll(centre, 7, 0)),
            jnp.where(spot == 0, before[i : i + 1], pltpu.roll(centre, 1, 0)),
        )
        num = jnp.zeros_like(centre)
        den = jnp.zeros_like(centre)
        for q in beside:
            edge_weight = 1.0 / (jnp.abs(centre - q) + tv_edge)
            num = num + edge_weight * q
            den = den + edge_weight * centre
        tv_num_ref[8 * i : 8 * i + 8, :] = tv_strength * num
        tv_den_ref[8 * i : 8 * i + 8, :] = tv_strength * den


def project_kernel(
    tv_strength, where_ref, h_ref, keep_ref, got_ref, coarse_ref, edges_ref, w_ref, out_ref, tv_num_ref, tv_den_ref, wide_ref
):
    tile, lane = keep_ref.shape[1:]
    half_blocks = keep_ref.shape[0] - SPARE
    chunks = h_ref.shape[0]
    comps = 2 * chunks
    copies = out_ref.shape[0]
    core = where_ref[2]
    for j in range(ACROSS):
        block = h_ref[:, :, j * lane : (j + 1) * lane]
        wide_ref[j] = block.astype(F32).reshape(chunks * DEPTH, lane)

    def spectrum(b):
        parts = []
        for m in range(2):
            r, j = place_of(m * half_blocks + b)
            parts.append(wide_ref[j, pl.ds(r, chunks, stride=DEPTH), :])
        return jnp.concatenate(parts, axis=0).astype(BF16)

    total = jnp.zeros((2 * tile + comps, comps), F32)
    for b in range(0, half_blocks, 2):
        group = range(b, min(b + 2, half_blocks))
        h = jnp.concatenate([spectrum(i) for i in group], axis=1)
        own = jnp.concatenate([keep_ref[i] for i in group], axis=1)
        partner = jnp.concatenate([got_ref[i] for i in group], axis=1)
        total = total + nt(jnp.concatenate([own, partner, h], axis=0), h)
    name = component_of(iota((comps, lane), 0))
    to_low = jnp.where(iota((comps, lane), 1) == name, 1.0, 0.0)
    to_high = jnp.where(iota((comps, lane), 1) == name + comps, 1.0, 0.0)
    exact = dict(preferred_element_type=F32, precision=lax.Precision.HIGHEST)
    spec = lax.dot_general(to_low, total[2 * tile :], (((0,), (0,)), ((), ())), **exact)[:comps]
    spec = jnp.dot(spec, to_high, **exact)
    cross = jnp.dot(total[: 2 * tile], to_low, **exact)
    for to_core in range(2):
        both = spec + jnp.where(core == to_core, cross[:tile], cross[tile:])
        for i in range(copies // 2):
            out_ref[to_core * (copies // 2) + i] = both

    halo_row, halo_at = place_of(2 * half_blocks + 1)
    halos = []
    for n, (source, inside) in enumerate(rim_sources(where_ref, chunks)):
        rows = [
            h_ref[source, :, j * lane : (j + 1) * lane].astype(F32)[halo_row : halo_row + 1]
            for j in range(halo_at, halo_at + HALO)
        ]
        fine = unfold(jnp.concatenate(rows, axis=0))
        halos.append(jnp.where(inside, coarse_ref[8 * n : 8 * n + 8, :] + fine, 0.0))
    smooth(tv_strength, where_ref, *halos, edges_ref[...], w_ref, tv_num_ref, tv_den_ref)


def sum_kernel(parts_ref, out_ref):
    block = parts_ref[0]
    for i in range(1, parts_ref.shape[0]):
        block = block + parts_ref[i]
    out_ref[...] = block


def loadings_kernel(parts_ref, w_ref, tv_num_ref, tv_den_ref, out_ref):
    comps = w_ref.shape[1]
    block = parts_ref[0]
    for i in range(1, parts_ref.shape[0]):
        block = block + parts_ref[i]
    w = w_ref[...]
    fitted = jnp.dot(w, block, preferred_element_type=F32, precision=lax.Precision.HIGHEST)
    fitted = pltpu.roll(fitted, comps, 1)[:, :comps]
    out_ref[...] = w * (block[:, :comps] + tv_num_ref[...]) / (fitted + tv_den_ref[...])


def call(kernel, name, outs, in_specs, scratch=(), out_specs=None, cost=None):
    return pl.pallas_call(
        kernel,
        out_shape=tuple(jax.ShapeDtypeStruct(shape, dtype) for shape, dtype in outs),
        in_specs=in_specs,
        out_specs=out_specs or (vmem(),) * len(outs),
        scratch_shapes=scratch,
        cost_estimate=cost,
        compiler_params=params(),
        name=name,
    )


def local(spectra, block_ids, counts, loadings, components):
    tile_x, tile_y, slot_count, lane = spectra.shape
    tile = tile_x * tile_y
    comps = loadings.shape[2]
    slab_bins = components.shape[1]
    half_blocks = slab_bins // lane // 2
    half_bins = half_blocks * lane
    width = ACROSS * lane
    spots = [lax.axis_index(axis) for axis in (("y", "core"), "gy", "core", "y")]
    here = jnp.stack(spots).astype(jnp.int32)
    peers = ("y", "gy")
    chunks = lax.axis_size(peers)
    w = loadings.reshape(tile, comps)
    swap = [(0, 1), (1, 0)]
    tv_strength = tv_share * slab_bins * lax.axis_size(("w", "x"))

    in_hbm = [
        pltpu.with_memory_space_constraint(array, pltpu.HBM)
        for array in (block_ids.reshape(slot_count), w, spectra.transpose(0, 2, 1, 3))
    ]
    wide = ((ACROSS, chunks * DEPTH, lane), F32)
    keep, send, w = call(
        scatter_kernel,
        "scatter",
        [((half_blocks + SPARE, tile, lane), BF16)] * 2 + [((tile, comps), F32)],
        [smem(), smem(), anywhere(), anywhere(), anywhere()],
        [
            pltpu.SMEM((slot_count,), jnp.int32),
            pltpu.VMEM((tile_x, slot_count, tile_y, lane), BF16),
            pltpu.SemaphoreType.DMA((3,)),
        ],
    )(here, counts.reshape(1), *in_hbm)
    got = lax.ppermute(send, "core", swap)
    (own,) = call(
        own_kernel,
        "own",
        [wide],
        [vmem(), vmem()],
        cost=pl.CostEstimate(flops=2 * tile * comps * half_bins, bytes_accessed=4 * comps * half_bins, transcendentals=0),
    )(keep, w)
    codes, edges = call(
        numer_kernel,
        "numer",
        [((chunks, DEPTH, width), jnp.int16), ((16, comps), F32)],
        [smem(), vmem(), vmem(), vmem()],
        [pltpu.VMEM(*wide)],
    )(here, own, got, w)
    codes = lax.all_to_all(codes, peers, 0, 0, tiled=True)
    h_all, h_mine, h_send, coarse = call(
        spectra_kernel,
        "spectra",
        [((chunks, DEPTH, width), BF16), ((1, half_bins), F32), ((1, half_bins), F32), ((24, comps), F32)],
        [smem(), vmem(), vmem(), vmem(), vmem()],
        [pltpu.VMEM((1, half_bins), F32)] * 2,
    )(here, codes, edges, components, w)
    h_got = lax.ppermute(h_send, "core", swap)
    h_all = lax.all_to_all(h_all, peers, 0, 0, tiled=True)
    copies = lax.axis_size(("core", "x"))
    h_pair = jnp.concatenate([h_got, h_mine, h_got], axis=1)
    h_next = lax.dynamic_slice_in_dim(h_pair, (1 - lax.axis_index("core")) * half_bins, slab_bins, 1)
    h_all, h_next = lax.optimization_barrier((h_all, h_next))
    both, tv_num, tv_den = call(
        functools.partial(project_kernel, tv_strength),
        "project",
        [((copies, tile, 2 * comps), F32), ((tile, comps), F32), ((tile, comps), F32)],
        [smem()] + [vmem()] * 6,
        [pltpu.VMEM(*wide)],
    )(here, h_all, keep, got, coarse, edges, w)
    both = lax.all_to_all(both, ("core", "x"), 0, 0, tiled=True)
    (both,) = call(sum_kernel, "sum", [((tile, 2 * comps), F32)], [vmem()])(both)
    both = lax.all_gather(both, "w", axis=0)
    (w_next,) = call(loadings_kernel, "loadings", [((tile, comps), F32)], [vmem()] * 4)(both, w, tv_num, tv_den)
    return (w_next.reshape(tile_x, tile_y, comps), h_next)


def solution(mesh):
    gx, gy, mz = mesh.devices.shape
    fine = Mesh(mesh.devices.reshape(gx // 2, 2, gy, 4, mz // 4), ("y", "core", "gy", "w", "x"))
    rows, slabs = ("y", "core"), ("w", "x")
    in_specs = (
        P(rows, "gy", slabs, None),
        P(rows, "gy", slabs),
        P(rows, "gy", slabs),
        P(rows, "gy", None),
        P(None, slabs),
    )
    out_specs = (P(rows, "gy", None), P(("y", "core", "gy"), slabs))
    return jax.shard_map(local, mesh=fine, in_specs=in_specs, out_specs=out_specs, check_vma=False)
```

```python
import functools
import math
import jax
import jax.numpy as jnp
from jax import lax
from jax.experimental import pallas as pl
from jax.experimental.pallas import tpu as pltpu
from jax.sharding import Mesh, PartitionSpec as P

tv_edge = 0.1
tv_share = 0.1
LANE = 128
VMEM_LIMIT = 48 * 1024 * 1024
F32 = jnp.float32
BF16 = jnp.bfloat16


def params():
    return pltpu.CompilerParams(vmem_limit_bytes=VMEM_LIMIT)


def vmem():
    return pl.BlockSpec(memory_space=pltpu.VMEM)


def smem():
    return pl.BlockSpec(memory_space=pltpu.SMEM)


def iota(shape, dim):
    return lax.broadcasted_iota(jnp.int32, shape, dim)


def nt(a, b):
    return lax.dot_general(a, b, (((1,), (1,)), ((), ())), preferred_element_type=F32)


LOG_LOW = 3.25
LOG_STEPS = 5950.0
GRAM_SCALE = 64.0
OFFSET = 32768


def encode(value):
    steps = jnp.log2(jnp.maximum(value, 1.0)) * LOG_STEPS + (1.5 - LOG_LOW * LOG_STEPS)
    return jnp.maximum(steps, 0.0).astype(jnp.int32)


def decode(code):
    steps = code.astype(jnp.int32).astype(F32) + float(OFFSET)
    return jnp.where(steps > 0.0, jnp.exp2(steps * (1.0 / LOG_STEPS) + (LOG_LOW - 1.0 / LOG_STEPS)), 0.0)


ACROSS = 13
SPARE = 2
DEPTH = 8
HALO = 4


def place_of(q):
    return divmod(q, ACROSS)


def component_of(row):
    return 8 * (row % 32 // 4) + 4 * (row // 32) + row % 4


def anywhere():
    return pl.BlockSpec(memory_space=pl.ANY)


def fetch(pairs, sems):
    copies = [pltpu.make_async_copy(source, target, sems.at[i]) for i, (source, target) in enumerate(pairs)]
    for copy in copies:
        copy.start()
    return copies


def scatter_kernel(where_ref, count_ref, ids_hbm, w_hbm, x_hbm, keep_ref, send_ref, w_ref, ids_ref, x_ref, sems):
    copies = fetch([(x_hbm, x_ref), (ids_hbm, ids_ref), (w_hbm, w_ref)], sems)
    tile_x, slots, tile_y, lane = x_ref.shape
    tile = tile_x * tile_y
    half_blocks = keep_ref.shape[0] - SPARE
    spill = half_blocks + 1
    core, count = where_ref[2], count_ref[0]
    keep_ref[...] = jnp.zeros_like(keep_ref)
    send_ref[...] = jnp.zeros_like(send_ref)
    for copy in copies:
        copy.wait()
    w = w_ref[...]
    edges = jnp.concatenate([w[:8], w[tile - 8 :]], axis=0)
    high = edges.astype(BF16).astype(F32)
    mid = (edges - high).astype(BF16).astype(F32)
    pieces = jnp.concatenate([high, mid, edges - high - mid, jnp.zeros_like(edges)], axis=0)
    send_ref[half_blocks] = jnp.concatenate([w, pieces], axis=1).astype(BF16)

    def place(s):
        block = ids_ref[s]
        upper = block >= half_blocks
        at = jnp.where(s < count, jnp.where(upper, block - half_blocks, block), spill)
        rows_of_slot = x_ref[:, s].astype(F32).reshape(tile, lane).astype(BF16)
        here = upper == (core == 1)
        keep_ref[jnp.where(here, at, spill)] = rows_of_slot
        send_ref[jnp.where(here, spill, at)] = rows_of_slot

    def place_group(g, carry):
        for i in range(group):
            place(g * group + i)
        return carry

    group = math.gcd(slots, 4)
    lax.fori_loop(0, (count + group - 1) // group, place_group, 0)


def put(wide_ref, q, value):
    r, j = place_of(q)
    wide_ref[j, pl.ds(r, value.shape[0], stride=DEPTH), :] = value


def numerators(w_low, dense_ref, half_blocks, wide_ref):
    comps = w_low.shape[1]
    chunks = wide_ref.shape[1] // DEPTH
    lane = LANE
    pick = jnp.where(iota((comps, comps), 1) == component_of(iota((comps, comps), 0)), 1.0, 0.0).astype(BF16)
    left = nt(pick, w_low).astype(BF16)
    for b in range(0, half_blocks, 2):
        group = range(b, min(b + 2, half_blocks))
        right = jnp.concatenate([dense_ref[i] for i in group], axis=1)
        product = jnp.dot(left, right, preferred_element_type=F32)
        for i in group:
            for m in range(2):
                part = product[m * chunks : (m + 1) * chunks, (i - b) * lane : (i - b + 1) * lane]
                put(wide_ref, m * half_blocks + i, part)
    gram = jnp.dot(left, w_low, preferred_element_type=F32) * GRAM_SCALE
    put(wide_ref, 2 * half_blocks, jnp.concatenate([gram[:chunks], gram[chunks:]], axis=1))
    for q in range(2 * half_blocks + 1, ACROSS * DEPTH):
        put(wide_ref, q, jnp.zeros((chunks, lane), F32))


def own_kernel(keep_ref, w_ref, own_ref):
    numerators(w_ref[...].astype(BF16), keep_ref, keep_ref.shape[0] - SPARE, own_ref)


def rims(where_ref, w, edges):
    at_first = where_ref[2] == 0
    tile = w.shape[0]
    bottom = jnp.where(at_first, edges[8:], w[tile - 8 :])
    top = jnp.where(at_first, w[:8], edges[:8])
    first = jnp.concatenate([w[8 * i : 8 * i + 1] for i in range(8)], axis=0)
    last = jnp.concatenate([w[8 * i + 7 : 8 * i + 8] for i in range(8)], axis=0)
    return [jnp.concatenate([rim[:4], rim[4:]], axis=1) for rim in (bottom, top, last, first)]


def coarse_part(value):
    return (value * 32768.0 + 0.5).astype(jnp.int32)


def rim_for(i, where_ref, values):
    side, y = where_ref[1], where_ref[3]
    to_y, to_side = divmod(i, 4)
    same_side, same_y = side == to_side, y == to_y
    out = jnp.where(jnp.logical_and(same_side, y + 1 == to_y), values[0], jnp.zeros_like(values[0]))
    out = jnp.where(jnp.logical_and(same_side, y - 1 == to_y), values[1], out)
    out = jnp.where(jnp.logical_and(same_y, side + 1 == to_side), values[2], out)
    return jnp.where(jnp.logical_and(same_y, side - 1 == to_side), values[3], out)


def rim_sources(where_ref, chunks):
    side, core, y = where_ref[1], where_ref[2], where_ref[3]
    out = []
    for from_y, from_side in ((jnp.where(core == 0, y - 1, y + 1), side), (y, side - 1), (y, side + 1)):
        inside = jnp.logical_and(
            jnp.logical_and(from_y >= 0, from_y < chunks // 4), jnp.logical_and(from_side >= 0, from_side < 4)
        )
        out.append((jnp.where(inside, from_y * 4 + from_side, 0), inside))
    return out


def unfold(rows):
    half = rows.shape[1] // 2
    return jnp.concatenate([rows[:, :half], rows[:, half:]], axis=0)


def numer_kernel(where_ref, own_ref, got_ref, w_ref, codes_ref, edges_ref, wide_ref):
    half_blocks = got_ref.shape[0] - SPARE
    lane = LANE
    comps = w_ref.shape[1]
    chunks = codes_ref.shape[0]
    apart = got_ref[half_blocks]
    pieces = apart[:, comps:].astype(F32)
    edges = pieces[:16] + pieces[16:32] + pieces[32:48]
    edges_ref[...] = edges
    numerators(apart[:, :comps], got_ref, half_blocks, wide_ref)

    rim_values = [coarse_part(rim) for rim in rims(where_ref, w_ref[...], edges)]
    row = iota((DEPTH, lane), 0)
    halo_row, halo_at = place_of(2 * half_blocks + 1)
    for i in range(chunks):
        rim = rim_for(i, where_ref, rim_values)
        at = slice(i * DEPTH, (i + 1) * DEPTH)
        for j in range(ACROSS):
            code = encode(own_ref[j, at, :] + wide_ref[j, at, :])
            if halo_at <= j < halo_at + HALO:
                code = jnp.where(row == halo_row, rim[j - halo_at : j - halo_at + 1], code)
            codes_ref[i, :, j * lane : (j + 1) * lane] = (code - OFFSET).astype(jnp.int16)


def spectra_kernel(
    where_ref, codes_ref, edges_ref, comps_ref, w_ref, h_all_ref, mine_ref, send_ref, coarse_ref, first_ref, second_ref
):
    lane = LANE
    chunks = codes_ref.shape[0]
    tile, comps = w_ref.shape
    half_blocks = mine_ref.shape[1] // lane
    side, core, y = where_ref[1], where_ref[2], where_ref[3]
    turn = lax.rem(8 - side, 8)
    parts = (first_ref, second_ref)

    def total(j):
        block = slice(j * lane, (j + 1) * lane)
        out = decode(codes_ref[0, :, block])
        for i in range(1, chunks):
            out = out + decode(codes_ref[i, :, block])
        return out

    sums = [total(j) for j in range(ACROSS)]
    gram_row, gram_at = place_of(2 * half_blocks)
    gram = jnp.transpose(sums[gram_at])[:, gram_row : gram_row + 1] * (1.0 / GRAM_SCALE)
    grams = [jnp.broadcast_to(gram[m * comps : (m + 1) * comps], (comps, lane)) for m in range(2)]
    halo_row, halo_at = place_of(2 * half_blocks + 1)
    w = w_ref[...]
    rim_values = [rim - coarse_part(rim).astype(F32) * (1.0 / 32768.0) for rim in rims(where_ref, w, edges_ref[...])]
    rim_low = [rim_for(i, where_ref, rim_values) for i in range(chunks)]
    row = iota((DEPTH, lane), 0)
    for j in range(ACROSS):
        denominators, own_rows = [], []
        for r in range(DEPTH):
            q = r * ACROSS + j
            if q < 2 * half_blocks:
                m, b = divmod(q, half_blocks)
                at = pl.ds(pl.multiple_of((core * half_blocks + b) * lane, lane), lane)
                denominators.append(jnp.sum(comps_ref[:, at] * grams[m], axis=0, keepdims=True))
                group = comps_ref[pl.ds(pl.multiple_of(8 * y, 8), 8), at]
                own_rows.append(pltpu.roll(group, turn, 0)[4 * m : 4 * m + 1])
            else:
                denominators.append(jnp.ones((1, lane), F32))
                own_rows.append(jnp.zeros((1, lane), F32))
        h = jnp.concatenate(own_rows, axis=0) * sums[j] / jnp.concatenate(denominators, axis=0)
        for r in range(DEPTH):
            q = r * ACROSS + j
            if q < 2 * half_blocks:
                m, b = divmod(q, half_blocks)
                parts[m][:, b * lane : (b + 1) * lane] = h[r : r + 1]
        h_low = h.astype(BF16)
        for i in range(chunks):
            if halo_at <= j < halo_at + HALO:
                rim = rim_low[i][j - halo_at : j - halo_at + 1]
                h_low = jnp.where(row == halo_row, rim, h).astype(BF16)
            h_all_ref[i, :, j * lane : (j + 1) * lane] = h_low
    mine_ref[...] = jnp.where(core == 0, first_ref[...], second_ref[...])
    send_ref[...] = jnp.where(core == 0, second_ref[...], first_ref[...])

    for n, (source, inside) in enumerate(rim_sources(where_ref, chunks)):
        rows = [
            codes_ref[source, :, j * lane : (j + 1) * lane].astype(jnp.int32)[halo_row : halo_row + 1]
            for j in range(halo_at, halo_at + HALO)
        ]
        value = (jnp.concatenate(rows, axis=0) + OFFSET).astype(F32) * (1.0 / 32768.0)
        coarse_ref[8 * n : 8 * n + 8, :] = jnp.where(inside, unfold(value), 0.0)


def smooth(tv_strength, where_ref, outer, before, after, edges, w_ref, tv_num_ref, tv_den_ref):
    comps = w_ref.shape[1]
    at_first = where_ref[2] == 0
    above = jnp.where(at_first, outer, edges[8:])
    below = jnp.where(at_first, edges[:8], outer)
    spot = iota((8, comps), 0)
    rows = [w_ref[8 * i : 8 * i + 8, :] for i in range(8)]
    for i in range(8):
        centre = rows[i]
        beside = (
            rows[i + 1] if i < 7 else below,
            rows[i - 1] if i > 0 else above,
            jnp.where(spot == 7, after[i : i + 1], pltpu.roll(centre, 7, 0)),
            jnp.where(spot == 0, before[i : i + 1], pltpu.roll(centre, 1, 0)),
        )
        num = jnp.zeros_like(centre)
        den = jnp.zeros_like(centre)
        for q in beside:
            edge_weight = 1.0 / (jnp.abs(centre - q) + tv_edge)
            num = num + edge_weight * q
            den = den + edge_weight * centre
        tv_num_ref[8 * i : 8 * i + 8, :] = tv_strength * num
        tv_den_ref[8 * i : 8 * i + 8, :] = tv_strength * den


def project_kernel(
    tv_strength, where_ref, h_ref, keep_ref, got_ref, coarse_ref, edges_ref, w_ref, out_ref, tv_num_ref, tv_den_ref, wide_ref
):
    tile, lane = keep_ref.shape[1:]
    half_blocks = keep_ref.shape[0] - SPARE
    chunks = h_ref.shape[0]
    comps = 2 * chunks
    copies = out_ref.shape[0]
    core = where_ref[2]
    for j in range(ACROSS):
        block = h_ref[:, :, j * lane : (j + 1) * lane]
        wide_ref[j] = block.astype(F32).reshape(chunks * DEPTH, lane)

    def spectrum(b):
        parts = []
        for m in range(2):
            r, j = place_of(m * half_blocks + b)
            parts.append(wide_ref[j, pl.ds(r, chunks, stride=DEPTH), :])
        return jnp.concatenate(parts, axis=0).astype(BF16)

    total = jnp.zeros((2 * tile + comps, comps), F32)
    for b in range(0, half_blocks, 2):
        group = range(b, min(b + 2, half_blocks))
        h = jnp.concatenate([spectrum(i) for i in group], axis=1)
        own = jnp.concatenate([keep_ref[i] for i in group], axis=1)
        partner = jnp.concatenate([got_ref[i] for i in group], axis=1)
        total = total + nt(jnp.concatenate([own, partner, h], axis=0), h)
    name = component_of(iota((comps, lane), 0))
    to_low = jnp.where(iota((comps, lane), 1) == name, 1.0, 0.0).astype(BF16)

    def pieces(value):
        high = value.astype(BF16)
        rest = value - high.astype(F32)
        mid = rest.astype(BF16)
        return [high, mid, (rest - mid.astype(F32)).astype(BF16)]

    rows = total.shape[0]
    moved = jnp.dot(jnp.concatenate(pieces(total), axis=0), to_low, preferred_element_type=F32)
    moved = moved[:rows] + moved[rows : 2 * rows] + moved[2 * rows :]
    cross = moved[: 2 * tile]
    spec = lax.dot_general(
        to_low,
        jnp.concatenate(pieces(moved[2 * tile :]), axis=1),
        (((0,), (0,)), ((), ())),
        preferred_element_type=F32,
    )[:comps]
    spec = pltpu.roll(spec[:, :lane] + spec[:, lane : 2 * lane] + spec[:, 2 * lane :], comps, 1)
    for to_core in range(2):
        both = spec + jnp.where(core == to_core, cross[:tile], cross[tile:])
        for i in range(copies // 2):
            out_ref[to_core * (copies // 2) + i] = both

    halo_row, halo_at = place_of(2 * half_blocks + 1)
    halos = []
    for n, (source, inside) in enumerate(rim_sources(where_ref, chunks)):
        rows = [
            h_ref[source, :, j * lane : (j + 1) * lane].astype(F32)[halo_row : halo_row + 1]
            for j in range(halo_at, halo_at + HALO)
        ]
        fine = unfold(jnp.concatenate(rows, axis=0))
        halos.append(jnp.where(inside, coarse_ref[8 * n : 8 * n + 8, :] + fine, 0.0))
    smooth(tv_strength, where_ref, *halos, edges_ref[...], w_ref, tv_num_ref, tv_den_ref)


def sum_kernel(parts_ref, out_ref):
    block = parts_ref[0]
    for i in range(1, parts_ref.shape[0]):
        block = block + parts_ref[i]
    out_ref[...] = block


def loadings_kernel(parts_ref, w_ref, tv_num_ref, tv_den_ref, out_ref):
    comps = w_ref.shape[1]
    block = parts_ref[0]
    for i in range(1, parts_ref.shape[0]):
        block = block + parts_ref[i]
    w = w_ref[...]
    fitted = jnp.dot(w, block, preferred_element_type=F32, precision=lax.Precision.HIGHEST)
    fitted = pltpu.roll(fitted, comps, 1)[:, :comps]
    out_ref[...] = w * (block[:, :comps] + tv_num_ref[...]) / (fitted + tv_den_ref[...])


def call(kernel, name, outs, in_specs, scratch=(), out_specs=None, cost=None):
    return pl.pallas_call(
        kernel,
        out_shape=tuple(jax.ShapeDtypeStruct(shape, dtype) for shape, dtype in outs),
        in_specs=in_specs,
        out_specs=out_specs or (vmem(),) * len(outs),
        scratch_shapes=scratch,
        cost_estimate=cost,
        compiler_params=params(),
        name=name,
    )


def local(spectra, block_ids, counts, loadings, components):
    tile_x, tile_y, slot_count, lane = spectra.shape
    tile = tile_x * tile_y
    comps = loadings.shape[2]
    slab_bins = components.shape[1]
    half_blocks = slab_bins // lane // 2
    half_bins = half_blocks * lane
    width = ACROSS * lane
    spots = [lax.axis_index(axis) for axis in (("y", "core"), "gy", "core", "y")]
    here = jnp.stack(spots).astype(jnp.int32)
    peers = ("y", "gy")
    chunks = lax.axis_size(peers)
    w = loadings.reshape(tile, comps)
    swap = [(0, 1), (1, 0)]
    tv_strength = tv_share * slab_bins * lax.axis_size(("w", "x"))

    in_hbm = [
        pltpu.with_memory_space_constraint(array, pltpu.HBM)
        for array in (block_ids.reshape(slot_count), w, spectra.transpose(0, 2, 1, 3))
    ]
    wide = ((ACROSS, chunks * DEPTH, lane), F32)
    keep, send, w = call(
        scatter_kernel,
        "scatter",
        [((half_blocks + SPARE, tile, lane), BF16)] * 2 + [((tile, comps), F32)],
        [smem(), smem(), anywhere(), anywhere(), anywhere()],
        [
            pltpu.SMEM((slot_count,), jnp.int32),
            pltpu.VMEM((tile_x, slot_count, tile_y, lane), BF16),
            pltpu.SemaphoreType.DMA((3,)),
        ],
    )(here, counts.reshape(1), *in_hbm)
    got = lax.ppermute(send, "core", swap)
    (own,) = call(
        own_kernel,
        "own",
        [wide],
        [vmem(), vmem()],
        cost=pl.CostEstimate(flops=2 * tile * comps * half_bins, bytes_accessed=4 * comps * half_bins, transcendentals=0),
    )(keep, w)
    codes, edges = call(
        numer_kernel,
        "numer",
        [((chunks, DEPTH, width), jnp.int16), ((16, comps), F32)],
        [smem(), vmem(), vmem(), vmem()],
        [pltpu.VMEM(*wide)],
    )(here, own, got, w)
    codes = lax.all_to_all(codes, peers, 0, 0, tiled=True)
    h_all, h_mine, h_send, coarse = call(
        spectra_kernel,
        "spectra",
        [((chunks, DEPTH, width), BF16), ((1, half_bins), F32), ((1, half_bins), F32), ((24, comps), F32)],
        [smem(), vmem(), vmem(), vmem(), vmem()],
        [pltpu.VMEM((1, half_bins), F32)] * 2,
    )(here, codes, edges, components, w)
    h_got = lax.ppermute(h_send, "core", swap)
    h_all = lax.all_to_all(h_all, peers, 0, 0, tiled=True)
    copies = lax.axis_size(("core", "x"))
    h_pair = jnp.concatenate([h_got, h_mine, h_got], axis=1)
    h_next = lax.dynamic_slice_in_dim(h_pair, (1 - lax.axis_index("core")) * half_bins, slab_bins, 1)
    h_all, h_next = lax.optimization_barrier((h_all, h_next))
    both, tv_num, tv_den = call(
        functools.partial(project_kernel, tv_strength),
        "project",
        [((copies, tile, 2 * comps), F32), ((tile, comps), F32), ((tile, comps), F32)],
        [smem()] + [vmem()] * 6,
        [pltpu.VMEM(*wide)],
    )(here, h_all, keep, got, coarse, edges, w)
    both = lax.all_to_all(both, ("core", "x"), 0, 0, tiled=True)
    (both,) = call(sum_kernel, "sum", [((tile, 2 * comps), F32)], [vmem()])(both)
    both = lax.all_gather(both, "w", axis=0)
    (w_next,) = call(loadings_kernel, "loadings", [((tile, comps), F32)], [vmem()] * 4)(both, w, tv_num, tv_den)
    return (w_next.reshape(tile_x, tile_y, comps), h_next)


def solution(mesh):
    gx, gy, mz = mesh.devices.shape
    fine = Mesh(mesh.devices.reshape(gx // 2, 2, gy, 4, mz // 4), ("y", "core", "gy", "w", "x"))
    rows, slabs = ("y", "core"), ("w", "x")
    in_specs = (
        P(rows, "gy", slabs, None),
        P(rows, "gy", slabs),
        P(rows, "gy", slabs),
        P(rows, "gy", None),
        P(None, slabs),
    )
    out_specs = (P(rows, "gy", None), P(("y", "core", "gy"), slabs))
    return jax.shard_map(local, mesh=fine, in_specs=in_specs, out_specs=out_specs, check_vma=False)
```
